512 devices in a mesh: loop: 32 (over y, z_hi), grp: 16 (over z_lo, x, core).
Axes of the slice: x: 4, y: 8, z: 8 (z_hi: 4, z_lo: 2; z = z_hi * 2 + z_lo), core: 2. Of those that a mesh axis runs over, the one named last changes fastest.
Arguments:
- real_pool: bfloat16 [32, 16, 4, 32, 64], P('loop', 'grp'), may hold values from -6 to 6
- real_pick: int32 [32, 16, 2, 1], P('loop', 'grp'), may hold values from 0 to 3
- noise_latents: bfloat16 [32, 2, 128, 512], P('loop', None, None, 'grp'), may hold values from -6 to 6
- generator_in: float32 [32, 256, 128], P('loop'), may hold values from -0.5 to 0.5
- generator_out: float32 [32, 32, 256], P('loop'), may hold values from -0.375 to 0.375
- critic_lift: float32 [32, 16, 256, 32], P('loop', 'grp'), may hold values from -1 to 1
- critic_kernel: float32 [32, 16, 256, 2304], P('loop', 'grp'), may hold values from -0.125 to 0.125
- critic_head: float32 [32, 16, 256], P('loop', 'grp'), may hold values from -0.375 to 0.375
Outputs:
- updated_lift: float32 [32, 16, 256, 32], P('loop', 'grp')
- updated_kernel: float32 [32, 16, 256, 2304], P('loop', 'grp')
- updated_head: float32 [32, 16, 256], P('loop', 'grp')
- updated_first: float32 [32, 256, 128], P('loop')
- updated_second: float32 [32, 32, 256], P('loop')
- fake_gradient: float32 [32, 32, 512], P('loop', None, 'grp')
- real_scores: float32 [32, 16, 2, 1], P('loop', 'grp')
The draws below stay inside these ranges and needn't reach their ends.
All inputs are finite; a program needn't handle non-finite values.
Results may differ from the reference program's by a relative error of at most 0.023.
Values may be sent and summed in bfloat16 or wider, within the bound.
No kernel may reach another device: no remote copies, remote signals or barrier semaphores. Data moves between devices by JAX's collectives and lax.ppermute only.
A program may use at most 64 MiB of HBM per device.

```python
import math
import jax
import jax.numpy as jnp
from jax import lax

C = 32
CH = 256
ZD = 128
GH = 256
IMG_H = 8
IMG_W = 8
CELLS = 64
REAL_DEV = 1
POOL = 4
ROUNDS = 2
GROUP_CELLS = 512
N_LOOP = 32
N_GRP = 16


def place_ends(values, rng, smallest, largest):
    longest = values.shape.index(max(values.shape))
    spots = []
    for shift in (0, 1):
        where = [jax.random.randint(jax.random.fold_in(rng, axis), (), 0, length) for axis, length in enumerate(values.shape)]
        where[longest] = (where[longest] + shift) % values.shape[longest]
        spots.append(tuple(where))
    return values.at[spots[0]].set(smallest).at[spots[1]].set(largest)


def steps_of(key, extent, cuts, smallest, top_value):
    factor_of = 1.0
    for dim, shards_of in cuts:
        heights = jax.random.uniform(jax.random.fold_in(jax.random.fold_in(key, 6), dim), (shards_of,), jnp.float32, smallest / len(cuts), top_value / len(cuts))
        factor_of = factor_of * jnp.repeat(jnp.exp(heights), extent[dim] // shards_of).reshape((-1,) + (1,) * (len(extent) - 1 - dim))
    return factor_of


def normal_values(stream_key, shape, deviation, most, cuts=(), kind=jnp.bfloat16):
    values = jax.random.normal(stream_key, shape, jnp.float32) * deviation
    if len(cuts) > 0:
        values = steps_of(stream_key, shape, cuts, -0.22, 0.18) * values
    return jnp.clip(values, min=-most, max=most).astype(kind)


def setup_inputs(seed: int = 0) -> dict:
    key_list = jax.random.split(jax.random.key(seed), 9)
    return {
        "real_pool": normal_values(key_list[0], (N_LOOP, N_GRP, POOL, C, CELLS), 1.0, 6.0, ((0, 32), (1, 16))),
        "real_pick": place_ends(jax.random.randint(key_list[1], (N_LOOP, N_GRP, ROUNDS, REAL_DEV), 0, POOL), jax.random.fold_in(key_list[1], 1), 0, POOL - 1).astype(jnp.int32),
        "noise_latents": normal_values(key_list[2], (N_LOOP, ROUNDS, ZD, GROUP_CELLS), 1.0, 6.0, ((0, 32), (3, 16))),
        "generator_in": normal_values(key_list[3], (N_LOOP, GH, ZD), ZD ** -0.5, 0.5, ((0, 32),), jnp.float32),
        "generator_out": normal_values(key_list[4], (N_LOOP, C, GH), GH ** -0.5, 0.375, ((0, 32),), jnp.float32),
        "critic_lift": normal_values(key_list[5], (N_LOOP, N_GRP, CH, C), C ** -0.5, 1.0, ((0, 32), (1, 16)), jnp.float32),
        "critic_kernel": normal_values(key_list[6], (N_LOOP, N_GRP, CH, 9 * CH), (9 * CH) ** -0.5, 0.125, ((0, 32), (1, 16)), jnp.float32),
        "critic_head": normal_values(key_list[7], (N_LOOP, N_GRP, CH), CH ** -0.5, 0.375, ((0, 32), (1, 16)), jnp.float32),
    }


critic_rate = 0.05
generator_rate = 0.2

def critic_scores(lift_weight, kernel_weight, head_weight, images):
    total = images.shape[1]
    image_count = total // CELLS
    lifted = jax.nn.silu(jnp.dot(lift_weight.astype(jnp.bfloat16), images, preferred_element_type=jnp.float32)).astype(jnp.bfloat16)
    channels = lifted.shape[0]
    planes = lifted.reshape(channels, image_count, IMG_H, IMG_W)
    padded = jnp.pad(planes, ((0, 0), (0, 0), (1, 1), (1, 1)))
    tap_list = [padded[:, :, row_shift:row_shift + IMG_H, col_shift:col_shift + IMG_W] for row_shift in range(3) for col_shift in range(3)]
    patches = jnp.stack(tap_list, 0).reshape(9 * channels, total)
    hidden = jax.nn.silu(jnp.dot(kernel_weight.astype(jnp.bfloat16), patches, preferred_element_type=jnp.float32))
    cell_scores = jnp.dot(head_weight, hidden, precision=lax.Precision.HIGHEST)
    return lax.optimization_barrier(jnp.sum(cell_scores.reshape(image_count, CELLS), axis=1)) / math.sqrt(CELLS)

def critic_step(lift_weight, kernel_weight, head_weight, fake_rows, real_rows):
    fake_count = fake_rows.shape[1] // CELLS

    def critic_loss(lift_arg, kernel_arg, head_arg, fake_wide):
        joined = jnp.concatenate([fake_wide.astype(jnp.bfloat16), real_rows], axis=1)
        scores = critic_scores(lift_arg, kernel_arg, head_arg, joined)
        return (jnp.mean(scores[:fake_count]) - jnp.mean(scores[fake_count:]), scores)
    _, back, scores = jax.vjp(critic_loss, lift_weight, kernel_weight, head_weight, fake_rows.astype(jnp.float32), has_aux=True)
    grad_lift, grad_kernel, grad_head, grad_fake = back(jnp.ones((), jnp.float32))
    updated = (lift_weight - critic_rate * grad_lift, kernel_weight - critic_rate * grad_kernel, head_weight - critic_rate * grad_head)
    return (updated, -fake_count * grad_fake, scores[fake_count:])

def generate(first_weight, second_weight, latents):
    inner = jnp.dot(first_weight, latents.astype(jnp.float32), precision=lax.Precision.HIGHEST)
    return jnp.dot(second_weight, jax.nn.silu(inner), precision=lax.Precision.HIGHEST)

def generator_grads(first_weight, second_weight, latents, pull_back):
    _, back = jax.vjp(lambda a, b: generate(a, b, latents), first_weight, second_weight)
    return back(pull_back)

def pick_images(pool_images, picks):
    chosen = jnp.take(pool_images, picks, axis=0)
    return jnp.transpose(chosen, (1, 0, 2)).reshape(chosen.shape[1], chosen.shape[0] * chosen.shape[2])

def reference(real_pool, real_pick, noise_latents, generator_in, generator_out, critic_lift, critic_kernel, critic_head):
    lift_all, kernel_all, head_all = (critic_lift, critic_kernel, critic_head)
    first_all, second_all = (generator_in, generator_out)
    group_ids = jnp.repeat(jnp.arange(N_LOOP, dtype=jnp.int32), N_GRP)
    pool_flat = real_pool.reshape(N_LOOP * N_GRP, POOL, C, CELLS)
    score_list = []
    summed = None
    for round_index in range(ROUNDS):
        latents_all = noise_latents[:, round_index]
        fakes = jax.vmap(generate)(first_all, second_all, latents_all).astype(jnp.bfloat16)
        picks = real_pick[:, :, round_index].reshape(N_LOOP * N_GRP, REAL_DEV)

        def single(item):
            lift_one, kernel_one, head_one, pool_one, pick_one, group_one = item
            fake_one = lax.dynamic_index_in_dim(fakes, group_one, 0, keepdims=False)
            return critic_step(lift_one, kernel_one, head_one, fake_one, pick_images(pool_one, pick_one))
        updated, contrib, scores = lax.map(single, (lift_all.reshape(N_LOOP * N_GRP, CH, C), kernel_all.reshape(N_LOOP * N_GRP, CH, 9 * CH), head_all.reshape(N_LOOP * N_GRP, CH), pool_flat, picks, group_ids))
        summed = lax.optimization_barrier(jnp.sum(contrib.reshape(N_LOOP, N_GRP, C, GROUP_CELLS), axis=1))
        grad_first, grad_second = jax.vmap(generator_grads)(first_all, second_all, latents_all, summed)
        first_all = first_all - generator_rate * grad_first
        second_all = second_all - generator_rate * grad_second
        lift_all = jnp.roll(updated[0].reshape(N_LOOP, N_GRP, CH, C), 1, axis=0)
        kernel_all = jnp.roll(updated[1].reshape(N_LOOP, N_GRP, CH, 9 * CH), 1, axis=0)
        head_all = jnp.roll(updated[2].reshape(N_LOOP, N_GRP, CH), 1, axis=0)
        score_list.append(scores.reshape(N_LOOP, N_GRP, REAL_DEV))
    real_scores = jnp.stack(score_list, axis=2)
    return (lift_all, kernel_all, head_all, first_all, second_all, summed, real_scores)
```

```python
import functools

import jax
import jax.numpy as jnp
from jax import lax
from jax.experimental import pallas as pl
from jax.experimental.pallas import tpu as pltpu
from jax.sharding import PartitionSpec as P

ROUNDS = 2
CELLS = 64
C = 32
CH = 256
TAPS = 9
N_GRP = 16
FAKE = 512
ROWS = 576
WIDE = 640
KW = TAPS * CH

critic_rate = 0.05
generator_rate = 0.2

bf16 = jnp.bfloat16
f32 = jnp.float32
NN = (((1,), (0,)), ((), ()))
NT = (((1,), (1,)), ((), ()))


def dot(a, b, dims=NN):
    return lax.dot_general(a, b, dims, preferred_element_type=f32)


def exact_dot(a, b, dims=NN):
    return lax.dot_general(a, b, dims, precision=lax.Precision.HIGHEST, preferred_element_type=f32)


def sigmoid(x):
    return 1.0 / (1.0 + jnp.exp(-x))


def row_ids(width):
    return lax.broadcasted_iota(jnp.int32, (ROWS, width), 0)


def move_rows(x, by):
    if by == 0:
        return x
    pad = jnp.zeros((abs(by), x.shape[1]), x.dtype)
    if by > 0:
        return jnp.concatenate([x[by:], pad], axis=0)
    return jnp.concatenate([pad, x[:by]], axis=0)


def masks():
    rows = row_ids(CH)
    col = rows & 7
    row = (rows >> 3) & 7
    reads_x = {-1: col > 0, 1: col < 7}
    reads_y = {-1: row > 0, 1: row < 7}
    return reads_x, reads_y


def critic_forward(images, lift_t, kernel_of, head, patch_ref):
    reads_x, reads_y = masks()
    images_t = jnp.transpose(images.astype(f32))[:ROWS].astype(bf16)
    pre = dot(images_t, lift_t)
    gate = sigmoid(pre)
    lifted = (pre * gate).astype(bf16).astype(f32)
    slope = gate * (1.0 + pre * (1.0 - gate))
    z = None
    for b in range(3):
        dx = b - 1
        across = lifted
        if dx:
            across = jnp.where(reads_x[dx], pltpu.roll(lifted, (-dx) % ROWS, 0), 0.0)
        for a in range(3):
            dy = a - 1
            tap = move_rows(across, 8 * dy)
            if dy:
                tap = jnp.where(reads_y[dy], tap, 0.0)
            tap = tap.astype(bf16)
            patch_ref[3 * a + b] = tap
            part = dot(tap, kernel_of(3 * a + b), NT)
            z = part if z is None else z + part
    gate = sigmoid(z)
    hidden = z * gate
    weight = jnp.where(row_ids(CH) < FAKE, 1.0 / 64.0, -1.0 / 8.0)
    real_score = jnp.sum(hidden[FAKE:] * head, keepdims=True) / 8.0
    head_grad = jnp.sum(weight * hidden, axis=0, keepdims=True)
    z_grad = (weight * head) * (gate * (1.0 + z * (1.0 - gate)))
    return slope, z_grad, head_grad, real_score


def lift_pullback(slope, z_grad, kernel_of):
    reads_x, reads_y = masks()
    total = None
    for b in range(3):
        dx = b - 1
        across = None
        for a in range(3):
            dy = a - 1
            tap = dot(z_grad, kernel_of(3 * a + b))
            if dy:
                tap = jnp.where(reads_y[dy], tap, 0.0)
            tap = move_rows(tap, -8 * dy)
            across = tap if across is None else across + tap
        if dx:
            across = pltpu.roll(jnp.where(reads_x[dx], across, 0.0), dx % ROWS, 0)
        total = across if total is None else total + across
    return (total * slope).astype(bf16)


def real_image(pool_ref, pick_ref, round_index):
    return pool_ref[pick_ref[round_index]]


def latents_of(noise_ref, round_index):
    return noise_ref[:, C * round_index : C * (round_index + 1), :].reshape(FAKE, 128).astype(f32)


def put_images(images_ref, fakes, real):
    images_ref[:, :FAKE] = fakes.astype(bf16)
    images_ref[:, FAKE:] = jnp.concatenate([real, jnp.zeros_like(real)], axis=1)


def generate_kernel(pick_ref, noise_ref, first_ref, second_ref, pool_ref, lift_ref, head_ref, packed_in, packed_ref, images_ref):
    latents = latents_of(noise_ref, 0)
    inner = exact_dot(latents, first_ref[...], NT)
    fakes = exact_dot(second_ref[...], inner * sigmoid(inner), NT)
    put_images(images_ref, fakes, real_image(pool_ref, pick_ref, 0))
    packed_ref[:, :WIDE] = images_ref[:16]
    packed_ref[:, WIDE : 2 * WIDE] = images_ref[16:]
    lift = lift_ref[...].astype(bf16)
    packed_ref[:, 1280:1536] = lift[:16]
    packed_ref[:, 1536:1792] = lift[16:]
    packed_ref[:, 1792:2048] = jnp.broadcast_to(head_ref[...], (16, CH)).astype(bf16)
    packed_ref[:, 2048:] = jnp.zeros((16, KW - 2048), bf16)


def first_step_kernel(images_ref, lift_ref, kernel_ref, head_ref, copies_ref, lift_out, kernel_out, head_out, score_out, patch_ref, half_ref):
    for t in range(TAPS):
        half_ref[t] = kernel_ref[:, CH * t : CH * (t + 1)].astype(bf16)
    lift = lift_ref[...]
    head = head_ref[...]
    lift_half = lift.astype(bf16)
    images = images_ref[...]
    slope, z_grad, head_grad, score = critic_forward(images, lift_half, lambda t: half_ref[t], head, patch_ref)
    z_half = z_grad.astype(bf16)
    pre_grad = lift_pullback(slope, z_half, lambda t: half_ref[t])
    pull = (-8.0 * dot(lift_half, pre_grad, NT)[:, :FAKE]).astype(bf16)
    for j in range(N_GRP):
        copies_ref[j] = pull
    lift_out[...] = lift - critic_rate * dot(images[:, :ROWS], pre_grad)
    head_out[...] = head - critic_rate * head_grad
    z_turned = jnp.transpose(z_grad).astype(bf16)
    for t in range(TAPS):
        cols = slice(CH * t, CH * (t + 1))
        kernel_out[:, cols] = (kernel_ref[:, cols] - critic_rate * dot(z_turned, patch_ref[t])).astype(bf16)
    score_out[...] = jnp.broadcast_to(score, (8, 128))


def pull_only_kernel(images_ref, lift_ref, kernel_ref, head_ref, pull_ref, patch_ref):
    lift_half = lift_ref[...].astype(bf16)
    kernel_of = lambda t: kernel_ref[:, CH * t : CH * (t + 1)]
    slope, z_grad, _, score = critic_forward(images_ref[...], lift_half, kernel_of, head_ref[...], patch_ref)
    pre_grad = lift_pullback(slope, z_grad.astype(bf16), kernel_of)
    pull_ref[:, :FAKE] = (-8.0 * dot(lift_half, pre_grad, NT)[:, :FAKE]).astype(bf16)
    high = score.astype(bf16)
    middle = (score - high.astype(f32)).astype(bf16)
    low = (score - high.astype(f32) - middle.astype(f32)).astype(bf16)
    lane = lax.broadcasted_iota(jnp.int32, (C, 128), 1)
    three = jnp.where(lane == 0, high.astype(f32), jnp.where(lane == 1, middle.astype(f32), jnp.where(lane == 2, low.astype(f32), 0.0)))
    pull_ref[:, FAKE:] = three.astype(bf16)


def moved_first_kernel(packed_ref, lift_out, kernel_out, head_out, patch_ref):
    images = jnp.concatenate([packed_ref[CH:, :WIDE], packed_ref[CH:, WIDE : 2 * WIDE]], axis=0)
    lift_half = jnp.concatenate([packed_ref[CH:, 1280:1536], packed_ref[CH:, 1536:1792]], axis=0)
    head = packed_ref[CH:, 1792:2048].astype(f32)[:1]
    kernel_of = lambda t: packed_ref[:CH, CH * t : CH * (t + 1)]
    slope, z_grad, head_grad, _ = critic_forward(images, lift_half, kernel_of, head, patch_ref)
    pre_grad = lift_pullback(slope, z_grad.astype(bf16), kernel_of)
    lift_out[...] = lift_half.astype(f32) - critic_rate * dot(images[:, :ROWS], pre_grad)
    head_out[...] = head - critic_rate * head_grad
    z_turned = jnp.transpose(z_grad).astype(bf16)
    for t in range(TAPS):
        kernel_out[:, CH * t : CH * (t + 1)] = kernel_of(t).astype(f32) - critic_rate * dot(z_turned, patch_ref[t])


def moved_second_kernel(images_ref, lift_ref, kernel_ref, head_ref, lift_out, kernel_out, head_out, patch_ref, half_ref):
    for t in range(TAPS):
        half_ref[t] = kernel_ref[:, CH * t : CH * (t + 1)].astype(bf16)
    lift = lift_ref[...]
    head = head_ref[...]
    images = images_ref[...]
    kernel_of = lambda t: half_ref[t]
    slope, z_grad, head_grad, _ = critic_forward(images, lift.astype(bf16), kernel_of, head, patch_ref)
    pre_grad = lift_pullback(slope, z_grad.astype(bf16), kernel_of)
    lift_out[...] = lift - critic_rate * dot(images[:, :ROWS], pre_grad)
    head_out[...] = head - critic_rate * head_grad
    z_turned = jnp.transpose(z_grad).astype(bf16)
    for t in range(TAPS):
        cols = slice(CH * t, CH * (t + 1))
        kernel_out[:, cols] = kernel_ref[:, cols] - critic_rate * dot(z_turned, patch_ref[t])


def generator_step(pulls_ref, latents, first, second):
    total = pulls_ref[0].astype(f32)
    for j in range(1, N_GRP):
        total = total + pulls_ref[j].astype(f32)
    inner = exact_dot(latents, first, NT)
    gate = sigmoid(inner)
    second_grad = exact_dot(total, inner * gate)
    inner_grad = exact_dot(jnp.transpose(total), second) * (gate * (1.0 + inner * (1.0 - gate)))
    first_grad = exact_dot(jnp.transpose(inner_grad), latents)
    return total, first - generator_rate * first_grad, second - generator_rate * second_grad


def middle_kernel(pick_ref, pulls_ref, noise_ref, first_ref, second_ref, pool_ref, images_ref, first_out, second_out):
    _, first, second = generator_step(pulls_ref, latents_of(noise_ref, 0), first_ref[...], second_ref[...])
    first_out[...] = first
    second_out[...] = second
    inner = exact_dot(latents_of(noise_ref, 1), first, NT)
    fakes = exact_dot(second, inner * sigmoid(inner), NT)
    put_images(images_ref, fakes, real_image(pool_ref, pick_ref, 1))


def last_kernel(place_ref, pulls_ref, noise_ref, first_ref, second_ref, first_out, second_out, own_out):
    total, first, second = generator_step(pulls_ref, latents_of(noise_ref, 1), first_ref[...], second_ref[...])
    first_out[...] = first
    second_out[...] = second
    own = jnp.zeros((C, C), f32)
    for j in range(N_GRP):
        own = own + jnp.where(place_ref[0] == j, total[:, C * j : C * (j + 1)], 0.0)
    own_out[...] = own


def vmem(*_):
    return pl.BlockSpec(memory_space=pltpu.VMEM)


def smem():
    return pl.BlockSpec(memory_space=pltpu.SMEM)


def call(kernel, name, outs, ins, scratch=(), scalars=0):
    return pl.pallas_call(
        kernel,
        name=name,
        out_shape=[jax.ShapeDtypeStruct(s, d) for s, d in outs],
        in_specs=[smem()] * scalars + [vmem()] * (len(ins) - scalars),
        out_specs=[vmem()] * len(outs),
        scratch_shapes=list(scratch),
        compiler_params=pltpu.CompilerParams(vmem_limit_bytes=40 * 1024 * 1024),
    )(*ins)


def shifted(value, steps):
    count = lax.axis_size("loop")
    return lax.ppermute(value, "loop", [(s, (s + steps) % count) for s in range(count)])


def swap(copies):
    return lax.all_to_all(copies, "grp", 0, 0)


PATCHES = pltpu.VMEM((TAPS, ROWS, CH), bf16)
HALVES = pltpu.VMEM((TAPS, CH, CH), bf16)


def per_device(real_pool, real_pick, noise_latents, generator_in, generator_out, critic_lift, critic_kernel, critic_head):
    pool = real_pool[0, 0]
    pick = real_pick[0, 0, :, 0]
    first, second = generator_in[0], generator_out[0]
    lift = jnp.swapaxes(critic_lift[0, 0], 0, 1)
    kernel = critic_kernel[0, 0]
    head = critic_head[0, 0][None]

    own_noise = jnp.swapaxes(noise_latents[0], 1, 2).reshape(ROUNDS * C, 128)
    noise = swap(jnp.broadcast_to(own_noise[None], (N_GRP,) + own_noise.shape))

    packed = jnp.pad(kernel.astype(bf16), ((0, 16), (0, 0)))
    packed, images = pl.pallas_call(
        generate_kernel,
        name="make_fakes",
        grid=(1,),
        out_shape=[jax.ShapeDtypeStruct((CH + 16, KW), bf16), jax.ShapeDtypeStruct((C, WIDE), bf16)],
        in_specs=[smem()] + [vmem()] * 6 + [pl.BlockSpec(memory_space=pl.ANY)],
        out_specs=[pl.BlockSpec((16, KW), lambda i: (CH // 16, 0)), vmem()],
        input_output_aliases={7: 0},
        compiler_params=pltpu.CompilerParams(vmem_limit_bytes=40 * 1024 * 1024),
    )(pick, noise, first, second, pool, lift, head, packed)

    moved = shifted(packed, 2)

    copies, lift_1, kernel_1, head_1, score_0 = call(
        first_step_kernel,
        "first_step",
        [((N_GRP, C, FAKE), bf16), ((C, CH), f32), ((CH, KW), bf16), ((1, CH), f32), ((8, 128), f32)],
        (images, lift, kernel, head),
        (PATCHES, HALVES),
    )
    pulls = swap(copies)
    own_images, first_1, second_1 = call(
        middle_kernel,
        "generator_step",
        [((C, WIDE), bf16), ((CH, 128), f32), ((C, CH), f32)],
        (pick, pulls, noise, first, second, pool),
        scalars=1,
    )
    ahead_images = shifted(own_images, -1)
    (pull,) = call(pull_only_kernel, "second_pull", [((C, WIDE), bf16)], (ahead_images, lift_1, kernel_1, head_1), (PATCHES,))
    behind_images = shifted(own_images, 1)
    own_pull = shifted(pull, 1)
    pulls = swap(jnp.broadcast_to(own_pull[None, :, :FAKE], (N_GRP, C, FAKE)))

    moved_lift, moved_kernel, moved_head = call(
        moved_first_kernel, "moved_first", [((C, CH), f32), ((CH, KW), f32), ((1, CH), f32)], (moved,), (PATCHES,)
    )
    lift_2, kernel_2, head_2 = call(
        moved_second_kernel,
        "moved_second",
        [((C, CH), f32), ((CH, KW), f32), ((1, CH), f32)],
        (behind_images, moved_lift, moved_kernel, moved_head),
        (PATCHES, HALVES),
    )
    place = lax.axis_index("grp").astype(jnp.int32)[None]
    first_2, second_2, own_grad = call(
        last_kernel,
        "generator_last",
        [((CH, 128), f32), ((C, CH), f32), ((C, C), f32)],
        (place, pulls, noise, first_1, second_1),
        scalars=1,
    )
    score_1 = jnp.sum(own_pull[0, FAKE : FAKE + 3].astype(f32))
    scores = jnp.stack([score_0[0, 0], score_1])[:, None]
    return (
        jnp.swapaxes(lift_2, 0, 1)[None, None],
        kernel_2[None, None],
        head_2[0][None, None],
        first_2[None],
        second_2[None],
        own_grad[None],
        scores[None, None],
    )


def solution(mesh):
    return jax.shard_map(
        per_device,
        mesh=mesh,
        in_specs=(
            P("loop", "grp", None, None, None),
            P("loop", "grp", None, None),
            P("loop", None, None, "grp"),
            P("loop", None, None),
            P("loop", None, None),
            P("loop", "grp", None, None),
            P("loop", "grp", None, None),
            P("loop", "grp", None),
        ),
        out_specs=(
            P("loop", "grp", None, None),
            P("loop", "grp", None, None),
            P("loop", "grp", None),
            P("loop", None, None),
            P("loop", None, None),
            P("loop", None, "grp"),
            P("loop", "grp", None, None),
        ),
        check_vma=False,
    )
```

```python
import functools

import jax
import jax.numpy as jnp
from jax import lax
from jax.experimental import pallas as pl
from jax.experimental.pallas import tpu as pltpu
from jax.sharding import PartitionSpec as P

ROUNDS = 2
CELLS = 64
C = 32
CH = 256
TAPS = 9
N_GRP = 16
FAKE = 512
ROWS = 576
WIDE = 640
KW = TAPS * CH
PART_A = 96
PART_B = 80
PART_C = CH - PART_A - PART_B

critic_rate = 0.05
generator_rate = 0.2

bf16 = jnp.bfloat16
f32 = jnp.float32
NN = (((1,), (0,)), ((), ()))
NT = (((1,), (1,)), ((), ()))


def dot(a, b, dims=NN):
    return lax.dot_general(a, b, dims, preferred_element_type=f32)


def exact_dot(a, b, dims=NN):
    return lax.dot_general(a, b, dims, precision=lax.Precision.HIGHEST, preferred_element_type=f32)


def sigmoid(x):
    return 1.0 / (1.0 + jnp.exp(-x))


def row_ids(width):
    return lax.broadcasted_iota(jnp.int32, (ROWS, width), 0)


def move_rows(x, by):
    if by == 0:
        return x
    pad = jnp.zeros((abs(by), x.shape[1]), x.dtype)
    if by > 0:
        return jnp.concatenate([x[by:], pad], axis=0)
    return jnp.concatenate([pad, x[:by]], axis=0)


def masks():
    rows = row_ids(CH)
    col = rows & 7
    row = (rows >> 3) & 7
    reads_x = {-1: col > 0, 1: col < 7}
    reads_y = {-1: row > 0, 1: row < 7}
    return reads_x, reads_y


def critic_forward(images, lift_t, kernel_of, head, patch_ref):
    reads_x, reads_y = masks()
    images_t = jnp.transpose(images.astype(f32))[:ROWS].astype(bf16)
    pre = dot(images_t, lift_t)
    gate = sigmoid(pre)
    lifted = (pre * gate).astype(bf16).astype(f32)
    slope = gate * (1.0 + pre * (1.0 - gate))
    z = None
    for b in range(3):
        dx = b - 1
        across = lifted
        if dx:
            across = jnp.where(reads_x[dx], pltpu.roll(lifted, (-dx) % ROWS, 0), 0.0)
        for a in range(3):
            dy = a - 1
            tap = move_rows(across, 8 * dy)
            if dy:
                tap = jnp.where(reads_y[dy], tap, 0.0)
            tap = tap.astype(bf16)
            patch_ref[3 * a + b] = tap
            part = dot(tap, kernel_of(3 * a + b), NT)
            z = part if z is None else z + part
    gate = sigmoid(z)
    hidden = z * gate
    weight = jnp.where(row_ids(CH) < FAKE, 1.0 / 64.0, -1.0 / 8.0)
    real_score = jnp.sum(hidden[FAKE:] * head, keepdims=True) / 8.0
    head_grad = jnp.sum(weight * hidden, axis=0, keepdims=True)
    z_grad = (weight * head) * (gate * (1.0 + z * (1.0 - gate)))
    return slope, z_grad, head_grad, real_score


def lift_pullback(slope, z_grad, kernel_of):
    reads_x, reads_y = masks()
    total = None
    for b in range(3):
        dx = b - 1
        across = None
        for a in range(3):
            dy = a - 1
            tap = dot(z_grad, kernel_of(3 * a + b))
            if dy:
                tap = jnp.where(reads_y[dy], tap, 0.0)
            tap = move_rows(tap, -8 * dy)
            across = tap if across is None else across + tap
        if dx:
            across = pltpu.roll(jnp.where(reads_x[dx], across, 0.0), dx % ROWS, 0)
        total = across if total is None else total + across
    return (total * slope).astype(bf16)


def real_image(pool_ref, pick_ref, round_index):
    return pool_ref[pick_ref[round_index]]


def latents_of(noise_ref, round_index):
    halves = []
    for z in range(2):
        start = 2 * C * z + C * round_index
        halves.append(noise_ref[:, start : start + C, :].reshape(FAKE // 2, 128))
    return jnp.concatenate(halves, axis=0).astype(f32)


def put_images(images_ref, fakes, real):
    images_ref[:, :FAKE] = fakes.astype(bf16)
    images_ref[:, FAKE:] = jnp.concatenate([real, jnp.zeros_like(real)], axis=1)


def noise_copies_kernel(place_ref, own_ref, other_ref, copies_ref):
    own_first = place_ref[0] < 8
    own = own_ref[...].astype(f32)
    other = other_ref[...].astype(f32)
    low = jnp.where(own_first, own, other).astype(bf16)
    high = jnp.where(own_first, other, own).astype(bf16)
    for j in range(8):
        copies_ref[j, : 2 * C] = low
        copies_ref[j, 2 * C :] = high


def pair_copies_kernel(own_ref, other_ref, copies_ref):
    pair = (own_ref[...].astype(f32) + other_ref[...].astype(f32)).astype(bf16)
    for j in range(8):
        copies_ref[j] = pair


def sum_of(pulls_ref):
    total = pulls_ref[0].astype(f32)
    for j in range(1, 8):
        total = total + pulls_ref[j].astype(f32)
    return total


def sum_kernel(pulls_ref, score_ref, out_ref):
    out_ref[:, :FAKE] = sum_of(pulls_ref).astype(bf16)
    out_ref[:, FAKE:] = score_ref[...]


def generate_kernel(pick_ref, noise_ref, first_ref, second_ref, pool_ref, images_ref):
    latents = latents_of(noise_ref, 0)
    inner = exact_dot(latents, first_ref[...], NT)
    fakes = exact_dot(second_ref[...], inner * sigmoid(inner), NT)
    put_images(images_ref, fakes, real_image(pool_ref, pick_ref, 0))


def first_step_kernel(images_ref, lift_ref, kernel_ref, head_ref, pull_ref, lift_out, kernel_out, head_out, score_out, rest_out, patch_ref, half_ref):
    for t in range(TAPS):
        half_ref[t] = kernel_ref[:, CH * t : CH * (t + 1)].astype(bf16)
    lift = lift_ref[...]
    head = head_ref[...]
    lift_half = lift.astype(bf16)
    images = images_ref[...]
    slope, z_grad, head_grad, score = critic_forward(images, lift_half, lambda t: half_ref[t], head, patch_ref)
    z_half = z_grad.astype(bf16)
    pre_grad = lift_pullback(slope, z_half, lambda t: half_ref[t])
    pull_ref[...] = (-8.0 * dot(lift_half, pre_grad, NT)[:, :FAKE]).astype(bf16)
    lift_out[...] = lift - critic_rate * dot(images[:, :ROWS], pre_grad)
    head_out[...] = head - critic_rate * head_grad
    z_turned = jnp.transpose(z_grad).astype(bf16)
    for t in range(TAPS):
        cols = slice(CH * t, CH * (t + 1))
        kernel_out[:, cols] = (kernel_ref[:, cols] - critic_rate * dot(z_turned, patch_ref[t])).astype(bf16)
        rest_out[:PART_C, cols] = half_ref[t, CH - PART_C :, :]
    rest_out[PART_C:, :WIDE] = images[:16]
    rest_out[PART_C:, WIDE : 2 * WIDE] = images[16:]
    rest_out[PART_C:, 1280:1536] = lift_half[:16]
    rest_out[PART_C:, 1536:1792] = lift_half[16:]
    rest_out[PART_C:, 1792:2048] = jnp.broadcast_to(head, (16, CH)).astype(bf16)
    rest_out[PART_C:, 2048:] = jnp.zeros((16, KW - 2048), bf16)
    score_out[...] = jnp.broadcast_to(score, (8, 128))


def pull_only_kernel(images_ref, lift_ref, kernel_ref, head_ref, copies_ref, score_ref, patch_ref):
    lift_half = lift_ref[...].astype(bf16)
    kernel_of = lambda t: kernel_ref[:, CH * t : CH * (t + 1)]
    slope, z_grad, _, score = critic_forward(images_ref[...], lift_half, kernel_of, head_ref[...], patch_ref)
    pre_grad = lift_pullback(slope, z_grad.astype(bf16), kernel_of)
    pull = (-8.0 * dot(lift_half, pre_grad, NT)[:, :FAKE]).astype(bf16)
    for j in range(8):
        copies_ref[j] = pull
    high = score.astype(bf16)
    middle = (score - high.astype(f32)).astype(bf16)
    low = (score - high.astype(f32) - middle.astype(f32)).astype(bf16)
    lane = lax.broadcasted_iota(jnp.int32, (C, 128), 1)
    three = jnp.where(lane == 0, high.astype(f32), jnp.where(lane == 1, middle.astype(f32), jnp.where(lane == 2, low.astype(f32), 0.0)))
    score_ref[...] = three.astype(bf16)


def moved_first_kernel(part_a, part_b, part_c, lift_out, kernel_out, head_out, patch_ref, half_ref):
    for t in range(TAPS):
        cols = slice(CH * t, CH * (t + 1))
        half_ref[t, :PART_A] = part_a[:, cols]
        half_ref[t, PART_A : PART_A + PART_B] = part_b[:, cols]
        half_ref[t, PART_A + PART_B :] = part_c[:PART_C, cols]
    images = jnp.concatenate([part_c[PART_C:, :WIDE], part_c[PART_C:, WIDE : 2 * WIDE]], axis=0)
    lift_half = jnp.concatenate([part_c[PART_C:, 1280:1536], part_c[PART_C:, 1536:1792]], axis=0)
    head = part_c[PART_C:, 1792:2048].astype(f32)[:1]
    kernel_of = lambda t: half_ref[t]
    slope, z_grad, head_grad, _ = critic_forward(images, lift_half, kernel_of, head, patch_ref)
    pre_grad = lift_pullback(slope, z_grad.astype(bf16), kernel_of)
    lift_out[...] = lift_half.astype(f32) - critic_rate * dot(images[:, :ROWS], pre_grad)
    head_out[...] = head - critic_rate * head_grad
    z_turned = jnp.transpose(z_grad).astype(bf16)
    for t in range(TAPS):
        kernel_out[:, CH * t : CH * (t + 1)] = kernel_of(t).astype(f32) - critic_rate * dot(z_turned, patch_ref[t])


def moved_second_kernel(images_ref, lift_ref, kernel_ref, head_ref, lift_out, kernel_out, head_out, patch_ref, half_ref):
    for t in range(TAPS):
        half_ref[t] = kernel_ref[:, CH * t : CH * (t + 1)].astype(bf16)
    lift = lift_ref[...]
    head = head_ref[...]
    images = images_ref[...]
    kernel_of = lambda t: half_ref[t]
    slope, z_grad, head_grad, _ = critic_forward(images, lift.astype(bf16), kernel_of, head, patch_ref)
    pre_grad = lift_pullback(slope, z_grad.astype(bf16), kernel_of)
    lift_out[...] = lift - critic_rate * dot(images[:, :ROWS], pre_grad)
    head_out[...] = head - critic_rate * head_grad
    z_turned = jnp.transpose(z_grad).astype(bf16)
    for t in range(TAPS):
        cols = slice(CH * t, CH * (t + 1))
        kernel_out[:, cols] = kernel_ref[:, cols] - critic_rate * dot(z_turned, patch_ref[t])


def generator_step(total, latents, first, second):
    inner = exact_dot(latents, first, NT)
    gate = sigmoid(inner)
    second_grad = exact_dot(total, inner * gate)
    inner_grad = exact_dot(jnp.transpose(total), second) * (gate * (1.0 + inner * (1.0 - gate)))
    first_grad = exact_dot(jnp.transpose(inner_grad), latents)
    return first - generator_rate * first_grad, second - generator_rate * second_grad


def middle_kernel(pick_ref, pulls_ref, noise_ref, first_ref, second_ref, pool_ref, images_ref, first_out, second_out):
    first, second = generator_step(sum_of(pulls_ref), latents_of(noise_ref, 0), first_ref[...], second_ref[...])
    first_out[...] = first
    second_out[...] = second
    inner = exact_dot(latents_of(noise_ref, 1), first, NT)
    fakes = exact_dot(second, inner * sigmoid(inner), NT)
    put_images(images_ref, fakes, real_image(pool_ref, pick_ref, 1))


def last_kernel(place_ref, same_ref, cross_ref, noise_ref, first_ref, second_ref, score_ref, first_out, second_out, own_out, scores_out):
    total = same_ref[:, :FAKE].astype(f32) + cross_ref[:, :FAKE].astype(f32)
    first, second = generator_step(total, latents_of(noise_ref, 1), first_ref[...], second_ref[...])
    first_out[...] = first
    second_out[...] = second
    own = jnp.zeros((C, C), f32)
    for j in range(N_GRP):
        own = own + jnp.where(place_ref[0] == j, total[:, C * j : C * (j + 1)], 0.0)
    own_out[...] = own
    scores_out[0, 0] = jnp.max(score_ref[...])
    scores_out[1, 0] = jnp.sum(same_ref[:, FAKE:].astype(f32)[:1])


def vmem(*_):
    return pl.BlockSpec(memory_space=pltpu.VMEM)


def smem():
    return pl.BlockSpec(memory_space=pltpu.SMEM)


def call(kernel, name, outs, ins, scratch=(), scalars=0):
    return pl.pallas_call(
        kernel,
        name=name,
        out_shape=[jax.ShapeDtypeStruct(s, d) for s, d in outs],
        in_specs=[smem()] * scalars + [vmem()] * (len(ins) - scalars),
        out_specs=[vmem()] * len(outs),
        scratch_shapes=list(scratch),
        compiler_params=pltpu.CompilerParams(vmem_limit_bytes=24 * 1024 * 1024),
    )(*ins)


def shifted(value, steps):
    count = lax.axis_size("loop")
    return lax.ppermute(value, "loop", [(s, (s + steps) % count) for s in range(count)])


def across(value):
    return lax.ppermute(value, "grp", [(m, m ^ 8) for m in range(N_GRP)])


def shifted_across(value, steps):
    count = lax.axis_size("loop")
    pairs = [(l * N_GRP + m, (l + steps) % count * N_GRP + (m ^ 8)) for l in range(count) for m in range(N_GRP)]
    return lax.ppermute(value, ("loop", "grp"), pairs)


def swap(copies):
    count = lax.axis_size("loop")
    groups = [[8 * i + j for j in range(8)] for i in range(2 * count)]
    return lax.all_to_all(copies, ("loop", "grp"), 0, 0, axis_index_groups=groups)


def together(*values):
    return lax.optimization_barrier(values)


PATCHES = pltpu.VMEM((TAPS, ROWS, CH), bf16)
HALVES = pltpu.VMEM((TAPS, CH, CH), bf16)


def per_device(real_pool, real_pick, noise_latents, generator_in, generator_out, critic_lift, critic_kernel, critic_head):
    pool = real_pool[0, 0]
    pick = real_pick[0, 0, :, 0]
    first, second = generator_in[0], generator_out[0]
    lift = jnp.swapaxes(critic_lift[0, 0], 0, 1)
    kernel = critic_kernel[0, 0]
    head = critic_head[0, 0][None]

    place = lax.axis_index("grp").astype(jnp.int32)[None]
    own_noise = jnp.swapaxes(noise_latents[0], 1, 2).reshape(ROUNDS * C, 128)
    other_noise = across(own_noise)
    part_a = kernel[:PART_A].astype(bf16)
    part_b = kernel[PART_A : PART_A + PART_B].astype(bf16)
    part_a, other_noise = together(part_a, other_noise)
    moved_a = shifted(part_a, 2)
    (copies,) = call(
        noise_copies_kernel, "noise_copies", [((8, 4 * C, 128), bf16)], (place, own_noise, other_noise), scalars=1
    )
    noise = swap(copies)
    (images,) = call(
        generate_kernel, "make_fakes", [((C, WIDE), bf16)], (pick, noise, first, second, pool), scalars=1
    )
    pull, lift_1, kernel_1, head_1, score_0, part_c = call(
        first_step_kernel,
        "first_step",
        [((C, FAKE), bf16), ((C, CH), f32), ((CH, KW), bf16), ((1, CH), f32), ((8, 128), f32), ((PART_C + 16, KW), bf16)],
        (images, lift, kernel, head),
        (PATCHES, HALVES),
    )
    pull, moved_a = together(pull, moved_a)
    other_pull = across(pull)
    part_b, other_pull = together(part_b, other_pull)
    moved_b = shifted(part_b, 2)
    (copies,) = call(pair_copies_kernel, "pair_copies", [((8, C, FAKE), bf16)], (pull, other_pull))
    pulls = swap(copies)
    own_images, first_1, second_1 = call(
        middle_kernel,
        "generator_step",
        [((C, WIDE), bf16), ((CH, 128), f32), ((C, CH), f32)],
        (pick, pulls, noise, first, second, pool),
        scalars=1,
    )
    own_images, moved_b = together(own_images, moved_b)
    ahead_images = shifted(own_images, -1)
    behind_images = shifted(own_images, 1)
    part_c, ahead_images, behind_images = together(part_c, ahead_images, behind_images)
    moved_c = shifted(part_c, 2)
    copies, score_1 = call(
        pull_only_kernel,
        "second_pull",
        [((8, C, FAKE), bf16), ((C, 128), bf16)],
        (ahead_images, lift_1, kernel_1, head_1),
        (PATCHES,),
    )
    (partial,) = call(sum_kernel, "sum_pulls", [((C, WIDE), bf16)], (swap(copies), score_1))
    partial, moved_c = together(partial, moved_c)
    same = shifted(partial, 1)
    cross = shifted_across(partial, 1)

    moved_lift, moved_kernel, moved_head = call(
        moved_first_kernel,
        "moved_first",
        [((C, CH), f32), ((CH, KW), f32), ((1, CH), f32)],
        (moved_a, moved_b, moved_c),
        (PATCHES, HALVES),
    )
    lift_2, kernel_2, head_2 = call(
        moved_second_kernel,
        "moved_second",
        [((C, CH), f32), ((CH, KW), f32), ((1, CH), f32)],
        (behind_images, moved_lift, moved_kernel, moved_head),
        (PATCHES, HALVES),
    )
    first_2, second_2, own_grad, scores = pl.pallas_call(
        last_kernel,
        name="generator_last",
        out_shape=[
            jax.ShapeDtypeStruct((CH, 128), f32),
            jax.ShapeDtypeStruct((C, CH), f32),
            jax.ShapeDtypeStruct((C, C), f32),
            jax.ShapeDtypeStruct((ROUNDS, 1), f32),
        ],
        in_specs=[smem()] + [vmem()] * 6,
        out_specs=[vmem()] * 3 + [smem()],
        compiler_params=pltpu.CompilerParams(vmem_limit_bytes=24 * 1024 * 1024),
    )(place, same, cross, noise, first_1, second_1, score_0)
    return (
        jnp.swapaxes(lift_2, 0, 1)[None, None],
        kernel_2[None, None],
        head_2[0][None, None],
        first_2[None],
        second_2[None],
        own_grad[None],
        scores[None, None],
    )


def solution(mesh):
    return jax.shard_map(
        per_device,
        mesh=mesh,
        in_specs=(
            P("loop", "grp", None, None, None),
            P("loop", "grp", None, None),
            P("loop", None, None, "grp"),
            P("loop", None, None),
            P("loop", None, None),
            P("loop", "grp", None, None),
            P("loop", "grp", None, None),
            P("loop", "grp", None),
        ),
        out_specs=(
            P("loop", "grp", None, None),
            P("loop", "grp", None, None),
            P("loop", "grp", None),
            P("loop", None, None),
            P("loop", None, None),
            P("loop", None, "grp"),
            P("loop", "grp", None, None),
        ),
        check_vma=False,
    )
```

```python
import functools

import jax
import jax.numpy as jnp
from jax import lax
from jax.experimental import pallas as pl
from jax.experimental.pallas import tpu as pltpu
from jax.sharding import PartitionSpec as P

ROUNDS = 2
CELLS = 64
C = 32
CH = 256
TAPS = 9
N_GRP = 16
FAKE = 512
ROWS = 576
WIDE = 640
KW = TAPS * CH
PART_A = 160
PART_B = CH - PART_A
FIRST_WORK = 20_000_000_000

critic_rate = 0.05
generator_rate = 0.2

bf16 = jnp.bfloat16
f32 = jnp.float32
NN = (((1,), (0,)), ((), ()))
NT = (((1,), (1,)), ((), ()))


def dot(a, b, dims=NN):
    return lax.dot_general(a, b, dims, preferred_element_type=f32)


def split(x):
    high = x.astype(bf16)
    return high, (x - high.astype(f32)).astype(bf16)


def exact_dot(a, b, dims=NN):
    if b.dtype == bf16:
        high, low = split(a)
        return dot(high, b, dims) + dot(low, b, dims)
    if a.dtype == bf16:
        high, low = split(b)
        return dot(a, high, dims) + dot(a, low, dims)
    a_high, a_low = split(a)
    b_high, b_low = split(b)
    return dot(a_high, b_high, dims) + (dot(a_high, b_low, dims) + dot(a_low, b_high, dims))


def sigmoid(x):
    return 1.0 / (1.0 + jnp.exp(-x))


def row_ids(width):
    return lax.broadcasted_iota(jnp.int32, (ROWS, width), 0)


def move_rows(x, by):
    if by == 0:
        return x
    pad = jnp.zeros((abs(by), x.shape[1]), x.dtype)
    if by > 0:
        return jnp.concatenate([x[by:], pad], axis=0)
    return jnp.concatenate([pad, x[:by]], axis=0)


def masks():
    rows = row_ids(CH)
    col = rows & 7
    row = (rows >> 3) & 7
    reads_x = {-1: col > 0, 1: col < 7}
    reads_y = {-1: row > 0, 1: row < 7}
    return reads_x, reads_y


def critic_forward(images, lift_t, kernel_of, head, patch_ref):
    reads_x, reads_y = masks()
    images_t = jnp.transpose(images.astype(f32))[:ROWS].astype(bf16)
    pre = dot(images_t, lift_t)
    gate = sigmoid(pre)
    lifted = (pre * gate).astype(bf16).astype(f32)
    slope = gate * (1.0 + pre * (1.0 - gate))
    z = None
    for b in range(3):
        dx = b - 1
        across = lifted
        if dx:
            across = jnp.where(reads_x[dx], pltpu.roll(lifted, (-dx) % ROWS, 0), 0.0)
        for a in range(3):
            dy = a - 1
            tap = move_rows(across, 8 * dy)
            if dy:
                tap = jnp.where(reads_y[dy], tap, 0.0)
            tap = tap.astype(bf16)
            patch_ref[3 * a + b] = tap
            part = dot(tap, kernel_of(3 * a + b), NT)
            z = part if z is None else z + part
    gate = sigmoid(z)
    hidden = z * gate
    weight = jnp.where(row_ids(CH) < FAKE, 1.0 / 64.0, -1.0 / 8.0)
    real_score = jnp.sum(hidden[FAKE:] * head, keepdims=True) / 8.0
    head_grad = jnp.sum(weight * hidden, axis=0, keepdims=True)
    z_grad = (weight * head) * (gate * (1.0 + z * (1.0 - gate)))
    return slope, z_grad, head_grad, real_score


def lift_pullback(slope, z_grad, kernel_of):
    reads_x, reads_y = masks()
    total = None
    for b in range(3):
        dx = b - 1
        across = None
        for a in range(3):
            dy = a - 1
            tap = dot(z_grad, kernel_of(3 * a + b))
            if dy:
                tap = jnp.where(reads_y[dy], tap, 0.0)
            tap = move_rows(tap, -8 * dy)
            across = tap if across is None else across + tap
        if dx:
            across = pltpu.roll(jnp.where(reads_x[dx], across, 0.0), dx % ROWS, 0)
        total = across if total is None else total + across
    return (total * slope).astype(bf16)


def real_image(pool_ref, pick_ref, round_index):
    return pool_ref[pick_ref[round_index]]


def latents_of(noise_ref, round_index):
    halves = []
    for z in range(2):
        start = 2 * C * z + C * round_index
        halves.append(noise_ref[:, start : start + C, :].reshape(FAKE // 2, 128))
    return jnp.concatenate(halves, axis=0)


def put_images(images_ref, fakes, real):
    images_ref[:, :FAKE] = fakes.astype(bf16)
    images_ref[:, FAKE:] = jnp.concatenate([real, jnp.zeros_like(real)], axis=1)


def noise_copies_kernel(place_ref, own_ref, other_ref, copies_ref):
    own_first = place_ref[0] < 8
    own = own_ref[...].astype(f32)
    other = other_ref[...].astype(f32)
    low = jnp.where(own_first, own, other).astype(bf16)
    high = jnp.where(own_first, other, own).astype(bf16)
    for j in range(8):
        copies_ref[j, : 2 * C] = low
        copies_ref[j, 2 * C :] = high


def sum_of(pulls_ref):
    total = pulls_ref[0].astype(f32)
    for j in range(1, 8):
        total = total + pulls_ref[j].astype(f32)
    return total


def sum_kernel(pulls_ref, out_ref):
    out_ref[...] = sum_of(pulls_ref).astype(bf16)


def scored_sum_kernel(pulls_ref, score_ref, out_ref):
    out_ref[:, :FAKE] = sum_of(pulls_ref).astype(bf16)
    out_ref[:, FAKE:] = score_ref[...]


def put_halves(block_ref, images):
    block_ref[:, :WIDE] = images[:16]
    block_ref[:, WIDE : 2 * WIDE] = images[16:]


def add_images_kernel(images_ref, part_ref, block_ref):
    put_halves(block_ref, images_ref[...])
    block_ref[:, 2 * WIDE :] = jnp.zeros((16, KW - 2 * WIDE), bf16)


def generate_kernel(pick_ref, noise_ref, first_ref, second_ref, pool_ref, images_ref):
    latents = latents_of(noise_ref, 0)
    inner = exact_dot(latents, first_ref[...], NT)
    fakes = exact_dot(second_ref[...], inner * sigmoid(inner), NT)
    put_images(images_ref, fakes, real_image(pool_ref, pick_ref, 0))


def first_step_kernel(images_ref, lift_ref, kernel_ref, head_ref, copies_ref, lift_out, kernel_out, head_out, score_out, rest_out, patch_ref, half_ref):
    for t in range(TAPS):
        half_ref[t] = kernel_ref[:, CH * t : CH * (t + 1)].astype(bf16)
    lift = lift_ref[...]
    head = head_ref[...]
    lift_half = lift.astype(bf16)
    images = images_ref[...]
    slope, z_grad, head_grad, score = critic_forward(images, lift_half, lambda t: half_ref[t], head, patch_ref)
    z_half = z_grad.astype(bf16)
    pre_grad = lift_pullback(slope, z_half, lambda t: half_ref[t])
    pull = (-8.0 * dot(lift_half, pre_grad, NT)[:, :FAKE]).astype(bf16)
    for j in range(8):
        copies_ref[j] = pull
    lift_out[...] = lift - critic_rate * dot(images[:, :ROWS], pre_grad)
    head_out[...] = head - critic_rate * head_grad
    z_turned = jnp.transpose(z_grad).astype(bf16)
    for t in range(TAPS):
        cols = slice(CH * t, CH * (t + 1))
        kernel_out[:, cols] = (kernel_ref[:, cols] - critic_rate * dot(z_turned, patch_ref[t])).astype(bf16)
        rest_out[:PART_B, cols] = half_ref[t, PART_A:, :]
    block = rest_out.at[PART_B : PART_B + 16]
    put_halves(block, images)
    block[:, 1280:1536] = lift_half[:16]
    block[:, 1536:1792] = lift_half[16:]
    block[:, 1792:2048] = jnp.broadcast_to(head, (16, CH)).astype(bf16)
    block[:, 2048:] = jnp.zeros((16, KW - 2048), bf16)
    score_out[...] = jnp.broadcast_to(score, (8, 128))


def pull_only_kernel(images_ref, lift_ref, kernel_ref, head_ref, copies_ref, score_ref, patch_ref):
    lift_half = lift_ref[...].astype(bf16)
    kernel_of = lambda t: kernel_ref[:, CH * t : CH * (t + 1)]
    slope, z_grad, _, score = critic_forward(images_ref[...], lift_half, kernel_of, head_ref[...], patch_ref)
    pre_grad = lift_pullback(slope, z_grad.astype(bf16), kernel_of)
    pull = (-8.0 * dot(lift_half, pre_grad, NT)[:, :FAKE]).astype(bf16)
    for j in range(8):
        copies_ref[j] = pull
    high = score.astype(bf16)
    middle = (score - high.astype(f32)).astype(bf16)
    low = (score - high.astype(f32) - middle.astype(f32)).astype(bf16)
    lane = lax.broadcasted_iota(jnp.int32, (C, 128), 1)
    three = jnp.where(lane == 0, high.astype(f32), jnp.where(lane == 1, middle.astype(f32), jnp.where(lane == 2, low.astype(f32), 0.0)))
    score_ref[...] = three.astype(bf16)


def moved_first_kernel(part_a, part_b, lift_out, kernel_out, head_out, patch_ref, half_ref):
    for t in range(TAPS):
        cols = slice(CH * t, CH * (t + 1))
        half_ref[t, :PART_A] = part_a[:, cols]
        half_ref[t, PART_A:] = part_b[:PART_B, cols]
    block = part_b.at[PART_B : PART_B + 16]
    images = jnp.concatenate([block[:, :WIDE], block[:, WIDE : 2 * WIDE]], axis=0)
    lift_half = jnp.concatenate([block[:, 1280:1536], block[:, 1536:1792]], axis=0)
    head = block[:, 1792:2048].astype(f32)[:1]
    kernel_of = lambda t: half_ref[t]
    slope, z_grad, head_grad, _ = critic_forward(images, lift_half, kernel_of, head, patch_ref)
    pre_grad = lift_pullback(slope, z_grad.astype(bf16), kernel_of)
    lift_out[...] = lift_half.astype(f32) - critic_rate * dot(images[:, :ROWS], pre_grad)
    head_out[...] = head - critic_rate * head_grad
    z_turned = jnp.transpose(z_grad).astype(bf16)
    for t in range(TAPS):
        kernel_out[:, CH * t : CH * (t + 1)] = kernel_of(t).astype(f32) - critic_rate * dot(z_turned, patch_ref[t])


def moved_second_kernel(part_b, lift_ref, kernel_ref, head_ref, lift_out, kernel_out, head_out, patch_ref, half_ref):
    for t in range(TAPS):
        half_ref[t] = kernel_ref[:, CH * t : CH * (t + 1)].astype(bf16)
    lift = lift_ref[...]
    head = head_ref[...]
    block = part_b.at[PART_B + 16 :]
    images = jnp.concatenate([block[:, :WIDE], block[:, WIDE : 2 * WIDE]], axis=0)
    kernel_of = lambda t: half_ref[t]
    slope, z_grad, head_grad, _ = critic_forward(images, lift.astype(bf16), kernel_of, head, patch_ref)
    pre_grad = lift_pullback(slope, z_grad.astype(bf16), kernel_of)
    lift_out[...] = lift - critic_rate * dot(images[:, :ROWS], pre_grad)
    head_out[...] = head - critic_rate * head_grad
    z_turned = jnp.transpose(z_grad).astype(bf16)
    for t in range(TAPS):
        cols = slice(CH * t, CH * (t + 1))
        kernel_out[:, cols] = kernel_ref[:, cols] - critic_rate * dot(z_turned, patch_ref[t])


def generator_step(total, latents, first, second):
    inner = exact_dot(latents, first, NT)
    gate = sigmoid(inner)
    second_grad = exact_dot(total, inner * gate)
    inner_grad = exact_dot(jnp.transpose(total), second) * (gate * (1.0 + inner * (1.0 - gate)))
    first_grad = exact_dot(jnp.transpose(inner_grad), latents)
    return first - generator_rate * first_grad, second - generator_rate * second_grad


def middle_kernel(pick_ref, own_ref, other_ref, noise_ref, first_ref, second_ref, pool_ref, images_ref, first_out, second_out):
    first, second = generator_step(own_ref[...].astype(f32) + other_ref[...].astype(f32), latents_of(noise_ref, 0), first_ref[...], second_ref[...])
    first_out[...] = first
    second_out[...] = second
    inner = exact_dot(latents_of(noise_ref, 1), first, NT)
    fakes = exact_dot(second, inner * sigmoid(inner), NT)
    put_images(images_ref, fakes, real_image(pool_ref, pick_ref, 1))


def last_kernel(place_ref, own_ref, other_ref, noise_ref, first_ref, second_ref, score_ref, first_out, second_out, own_out, scores_out):
    total = own_ref[:, :FAKE].astype(f32) + other_ref[:, :FAKE].astype(f32)
    first, second = generator_step(total, latents_of(noise_ref, 1), first_ref[...], second_ref[...])
    first_out[...] = first
    second_out[...] = second
    own = jnp.zeros((C, C), f32)
    for j in range(N_GRP):
        own = own + jnp.where(place_ref[0] == j, total[:, C * j : C * (j + 1)], 0.0)
    own_out[...] = own
    scores_out[0, 0] = jnp.max(score_ref[...])
    scores_out[1, 0] = jnp.sum(own_ref[:, FAKE:].astype(f32)[:1])


def vmem(*_):
    return pl.BlockSpec(memory_space=pltpu.VMEM)


def smem():
    return pl.BlockSpec(memory_space=pltpu.SMEM)


def call(kernel, name, outs, ins, scratch=(), scalars=0, work=0):
    return pl.pallas_call(
        kernel,
        name=name,
        out_shape=[jax.ShapeDtypeStruct(s, d) for s, d in outs],
        in_specs=[smem()] * scalars + [vmem()] * (len(ins) - scalars),
        out_specs=[vmem()] * len(outs),
        scratch_shapes=list(scratch),
        cost_estimate=pl.CostEstimate(flops=work, bytes_accessed=0, transcendentals=0) if work else None,
        compiler_params=pltpu.CompilerParams(vmem_limit_bytes=24 * 1024 * 1024),
    )(*ins)


def shifted(value, steps):
    count = lax.axis_size("loop")
    return lax.ppermute(value, "loop", [(s, (s + steps) % count) for s in range(count)])


def across(value):
    return lax.ppermute(value, "grp", [(m, m ^ 8) for m in range(N_GRP)])


def swap(copies):
    count = lax.axis_size("loop")
    groups = [[8 * i + j for j in range(8)] for i in range(2 * count)]
    return lax.all_to_all(copies, ("loop", "grp"), 0, 0, axis_index_groups=groups)


def together(*values):
    return lax.optimization_barrier(values)


PATCHES = pltpu.VMEM((TAPS, ROWS, CH), bf16)
HALVES = pltpu.VMEM((TAPS, CH, CH), bf16)


def per_device(real_pool, real_pick, noise_latents, generator_in, generator_out, critic_lift, critic_kernel, critic_head):
    pool = real_pool[0, 0]
    pick = real_pick[0, 0, :, 0]
    first, second = generator_in[0], generator_out[0]
    lift = jnp.swapaxes(critic_lift[0, 0], 0, 1)
    kernel = critic_kernel[0, 0]
    head = critic_head[0, 0][None]

    place = lax.axis_index("grp").astype(jnp.int32)[None]
    own_noise = jnp.swapaxes(noise_latents[0], 1, 2).reshape(ROUNDS * C, 128)
    other_noise = across(own_noise)
    part_a = kernel[:PART_A].astype(bf16)
    (copies,) = call(
        noise_copies_kernel, "noise_copies", [((8, 4 * C, 128), bf16)], (place, own_noise, other_noise), scalars=1
    )
    part_a, copies = together(part_a, copies)
    moved_a = shifted(part_a, 2)
    noise = swap(copies)
    (images,) = call(
        generate_kernel, "make_fakes", [((C, WIDE), bf16)], (pick, noise, first, second, pool), scalars=1
    )
    copies, lift_1, kernel_1, head_1, score_0, part_b = call(
        first_step_kernel,
        "first_step",
        [((8, C, FAKE), bf16), ((C, CH), f32), ((CH, KW), bf16), ((1, CH), f32), ((8, 128), f32), ((PART_B + 32, KW), bf16)],
        (images, lift, kernel, head),
        (PATCHES, HALVES),
        work=FIRST_WORK,
    )
    (partial,) = call(sum_kernel, "sum_first", [((C, FAKE), bf16)], (swap(copies),))
    partial, moved_a = together(partial, moved_a)
    other = across(partial)
    own_images, first_1, second_1 = call(
        middle_kernel,
        "generator_step",
        [((C, WIDE), bf16), ((CH, 128), f32), ((C, CH), f32)],
        (pick, partial, other, noise, first, second, pool),
        scalars=1,
    )
    ahead_images = shifted(own_images, -1)
    part_b = pl.pallas_call(
        add_images_kernel,
        name="add_images",
        grid=(1,),
        out_shape=jax.ShapeDtypeStruct((PART_B + 32, KW), bf16),
        in_specs=[vmem(), pl.BlockSpec(memory_space=pl.ANY)],
        out_specs=pl.BlockSpec((16, KW), lambda i: ((PART_B + 16) // 16, 0)),
        input_output_aliases={1: 0},
        compiler_params=pltpu.CompilerParams(vmem_limit_bytes=24 * 1024 * 1024),
    )(ahead_images, part_b)
    part_b, ahead_images = together(part_b, ahead_images)
    moved_b = shifted(part_b, 2)
    copies, score_1 = call(
        pull_only_kernel,
        "second_pull",
        [((8, C, FAKE), bf16), ((C, 128), bf16)],
        (ahead_images, lift_1, kernel_1, head_1),
        (PATCHES,),
    )
    (partial,) = call(scored_sum_kernel, "sum_second", [((C, WIDE), bf16)], (swap(copies), score_1))
    partial, moved_b = together(partial, moved_b)
    same = shifted(partial, 1)

    moved_lift, moved_kernel, moved_head = call(
        moved_first_kernel,
        "moved_first",
        [((C, CH), f32), ((CH, KW), f32), ((1, CH), f32)],
        (moved_a, moved_b),
        (PATCHES, HALVES),
    )
    moved_lift, same = together(moved_lift, same)
    cross = across(same)
    lift_2, kernel_2, head_2 = call(
        moved_second_kernel,
        "moved_second",
        [((C, CH), f32), ((CH, KW), f32), ((1, CH), f32)],
        (moved_b, moved_lift, moved_kernel, moved_head),
        (PATCHES, HALVES),
    )
    first_2, second_2, own_grad, scores = pl.pallas_call(
        last_kernel,
        name="generator_last",
        out_shape=[
            jax.ShapeDtypeStruct((CH, 128), f32),
            jax.ShapeDtypeStruct((C, CH), f32),
            jax.ShapeDtypeStruct((C, C), f32),
            jax.ShapeDtypeStruct((ROUNDS, 1), f32),
        ],
        in_specs=[smem()] + [vmem()] * 6,
        out_specs=[vmem()] * 3 + [smem()],
        compiler_params=pltpu.CompilerParams(vmem_limit_bytes=24 * 1024 * 1024),
    )(place, same, cross, noise, first_1, second_1, score_0)
    return (
        jnp.swapaxes(lift_2, 0, 1)[None, None],
        kernel_2[None, None],
        head_2.reshape(1, 1, CH),
        first_2[None],
        second_2[None],
        own_grad[None],
        scores[None, None],
    )


def solution(mesh):
    return jax.shard_map(
        per_device,
        mesh=mesh,
        in_specs=(
            P("loop", "grp", None, None, None),
            P("loop", "grp", None, None),
            P("loop", None, None, "grp"),
            P("loop", None, None),
            P("loop", None, None),
            P("loop", "grp", None, None),
            P("loop", "grp", None, None),
            P("loop", "grp", None),
        ),
        out_specs=(
            P("loop", "grp", None, None),
            P("loop", "grp", None, None),
            P("loop", "grp", None),
            P("loop", None, None),
            P("loop", None, None),
            P("loop", None, "grp"),
            P("loop", "grp", None, None),
        ),
        check_vma=False,
    )
```

```python
import functools

import jax
import jax.numpy as jnp
from jax import lax
from jax.experimental import pallas as pl
from jax.experimental.pallas import tpu as pltpu
from jax.sharding import PartitionSpec as P

ROUNDS = 2
CELLS = 64
C = 32
CH = 256
TAPS = 9
N_GRP = 16
FAKE = 512
ROWS = 576
WIDE = 640
KW = TAPS * CH
PART_A = 160
PART_B = CH - PART_A
EXTRA = 512
FIRST_WORK = 2_000_000_000
COPY_WORK = 4_000_000_000

critic_rate = 0.05
generator_rate = 0.2

bf16 = jnp.bfloat16
f32 = jnp.float32
NN = (((1,), (0,)), ((), ()))
NT = (((1,), (1,)), ((), ()))


def dot(a, b, dims=NN):
    return lax.dot_general(a, b, dims, preferred_element_type=f32)


def split(x):
    high = x.astype(bf16)
    return high, (x - high.astype(f32)).astype(bf16)


def exact_dot(a, b, dims=NN):
    if b.dtype == bf16:
        high, low = split(a)
        return dot(high, b, dims) + dot(low, b, dims)
    if a.dtype == bf16:
        high, low = split(b)
        return dot(a, high, dims) + dot(a, low, dims)
    a_high, a_low = split(a)
    b_high, b_low = split(b)
    return dot(a_high, b_high, dims) + (dot(a_high, b_low, dims) + dot(a_low, b_high, dims))


def sigmoid(x):
    return 1.0 / (1.0 + jnp.exp(-x))


def row_ids(width):
    return lax.broadcasted_iota(jnp.int32, (ROWS, width), 0)


def move_rows(x, by):
    if by == 0:
        return x
    pad = jnp.zeros((abs(by), x.shape[1]), x.dtype)
    if by > 0:
        return jnp.concatenate([x[by:], pad], axis=0)
    return jnp.concatenate([pad, x[:by]], axis=0)


def masks():
    rows = row_ids(CH)
    col = rows & 7
    row = (rows >> 3) & 7
    reads_x = {-1: col > 0, 1: col < 7}
    reads_y = {-1: row > 0, 1: row < 7}
    return reads_x, reads_y


def critic_forward(images, lift_t, kernel_of, head, patch_ref):
    reads_x, reads_y = masks()
    images_t = jnp.transpose(images.astype(f32))[:ROWS].astype(bf16)
    pre = dot(images_t, lift_t)
    gate = sigmoid(pre)
    lifted = (pre * gate).astype(bf16).astype(f32)
    slope = gate * (1.0 + pre * (1.0 - gate))
    z = None
    for b in range(3):
        dx = b - 1
        across = lifted
        if dx:
            across = jnp.where(reads_x[dx], pltpu.roll(lifted, (-dx) % ROWS, 0), 0.0)
        for a in range(3):
            dy = a - 1
            tap = move_rows(across, 8 * dy)
            if dy:
                tap = jnp.where(reads_y[dy], tap, 0.0)
            tap = tap.astype(bf16)
            patch_ref[3 * a + b] = tap
            part = dot(tap, kernel_of(3 * a + b), NT)
            z = part if z is None else z + part
    gate = sigmoid(z)
    hidden = z * gate
    weight = jnp.where(row_ids(CH) < FAKE, 1.0 / 64.0, -1.0 / 8.0)
    real_score = jnp.sum(hidden[FAKE:] * head, keepdims=True) / 8.0
    head_grad = jnp.sum(weight * hidden, axis=0, keepdims=True)
    z_grad = (weight * head) * (gate * (1.0 + z * (1.0 - gate)))
    return slope, z_grad, head_grad, real_score


def lift_pullback(slope, z_grad, kernel_of):
    reads_x, reads_y = masks()
    total = None
    for b in range(3):
        dx = b - 1
        across = None
        for a in range(3):
            dy = a - 1
            tap = dot(z_grad, kernel_of(3 * a + b))
            if dy:
                tap = jnp.where(reads_y[dy], tap, 0.0)
            tap = move_rows(tap, -8 * dy)
            across = tap if across is None else across + tap
        if dx:
            across = pltpu.roll(jnp.where(reads_x[dx], across, 0.0), dx % ROWS, 0)
        total = across if total is None else total + across
    return (total * slope).astype(bf16)


def real_image(pool_ref, pick_ref, round_index):
    return pool_ref[pick_ref[round_index]]


def latents_of(noise_ref, round_index):
    halves = []
    for z in range(2):
        start = 2 * C * z + C * round_index
        halves.append(noise_ref[:, start : start + C, :].reshape(FAKE // 2, 128))
    return jnp.concatenate(halves, axis=0)


def put_images(images_ref, fakes, real):
    images_ref[:, :FAKE] = fakes.astype(bf16)
    images_ref[:, FAKE:] = jnp.concatenate([real, jnp.zeros_like(real)], axis=1)


def stage_kernel(kernel_ref, first_ref, second_ref, pool_ref, lift_ref, head_ref, noise_ref, part_ref, first_out, second_out, pool_out, lift_out, head_out, noise_out):
    part_ref[...] = kernel_ref[...].astype(bf16)

    @pl.when(pl.program_id(0) == 0)
    def _():
        first_out[...] = first_ref[...]
        second_out[...] = second_ref[...]
        pool_out[...] = pool_ref[...]
        lift_out[...] = lift_ref[...]
        head_out[...] = head_ref[...]
        noise_out[...] = noise_ref[...]


def noise_copies_kernel(place_ref, own_ref, other_ref, copies_ref):
    own_first = place_ref[0] < 8
    own = own_ref[...].astype(f32)
    other = other_ref[...].astype(f32)
    low = jnp.where(own_first, own, other).astype(bf16)
    high = jnp.where(own_first, other, own).astype(bf16)
    for j in range(8):
        copies_ref[j, : 2 * C] = low
        copies_ref[j, 2 * C :] = high


def sum_of(pulls_ref):
    total = pulls_ref[0].astype(f32)
    for j in range(1, 8):
        total = total + pulls_ref[j].astype(f32)
    return total


def sum_kernel(pulls_ref, out_ref):
    out_ref[...] = sum_of(pulls_ref).astype(bf16)


def scored_sum_kernel(pulls_ref, score_ref, out_ref):
    out_ref[:, :FAKE] = sum_of(pulls_ref).astype(bf16)
    out_ref[:, FAKE:] = score_ref[...]


def add_images_kernel(images_ref, part_in, part_ref):
    part_ref[:, : KW + EXTRA] = part_in[...]
    images = images_ref[...]
    part_ref[C : 2 * C, KW:] = images[:, :FAKE]
    tails = jnp.concatenate([part_in[2 * C :, KW : KW + CELLS], images[:, FAKE : FAKE + CELLS]], axis=1)
    part_ref[2 * C :, KW : KW + 128] = tails


def moved_images(part_ref, which):
    start = CELLS * which
    tails = part_ref[2 * C : 3 * C, KW : KW + 128][:, start : start + CELLS]
    return jnp.concatenate([part_ref[C * which : C * (which + 1), KW:], tails, jnp.zeros_like(tails)], axis=1)


def generate_kernel(pick_ref, noise_ref, first_ref, second_ref, pool_ref, images_ref):
    latents = latents_of(noise_ref, 0)
    inner = exact_dot(latents, first_ref[...], NT)
    fakes = exact_dot(second_ref[...], inner * sigmoid(inner), NT)
    put_images(images_ref, fakes, real_image(pool_ref, pick_ref, 0))


def first_step_kernel(images_ref, lift_ref, kernel_ref, head_ref, copies_ref, lift_out, kernel_out, head_out, score_out, rest_out, patch_ref, half_ref):
    for t in range(TAPS):
        half_ref[t] = kernel_ref[:, CH * t : CH * (t + 1)].astype(bf16)
    lift = lift_ref[...]
    head = head_ref[...]
    lift_half = lift.astype(bf16)
    images = images_ref[...]
    slope, z_grad, head_grad, score = critic_forward(images, lift_half, lambda t: half_ref[t], head, patch_ref)
    z_half = z_grad.astype(bf16)
    pre_grad = lift_pullback(slope, z_half, lambda t: half_ref[t])
    pull = (-8.0 * dot(lift_half, pre_grad, NT)[:, :FAKE]).astype(bf16)
    for j in range(8):
        copies_ref[j] = pull
    lift_out[...] = lift - critic_rate * dot(images[:, :ROWS], pre_grad)
    head_out[...] = head - critic_rate * head_grad
    z_turned = jnp.transpose(z_grad).astype(bf16)
    for t in range(TAPS):
        cols = slice(CH * t, CH * (t + 1))
        kernel_out[:, cols] = (kernel_ref[:, cols] - critic_rate * dot(z_turned, patch_ref[t])).astype(bf16)
        rest_out[:, cols] = half_ref[t, PART_A:, :]
    rest_out[:C, KW:] = images[:, :FAKE]
    rest_out[C : 2 * C, KW:] = jnp.zeros((C, EXTRA), bf16)
    rest_out[2 * C :, KW : KW + 128] = images[:, FAKE:]
    rest_out[2 * C :, KW + 128 : KW + 384] = lift_half
    lane = jnp.concatenate([jnp.broadcast_to(head[:, :128], (16, 128)), jnp.broadcast_to(head[:, 128:], (16, 128))], axis=0)
    rest_out[2 * C :, KW + 384 :] = lane.astype(bf16)
    score_out[...] = jnp.broadcast_to(score, (8, 128))


def pull_only_kernel(images_ref, lift_ref, kernel_ref, head_ref, copies_ref, score_ref, patch_ref):
    lift_half = lift_ref[...].astype(bf16)
    kernel_of = lambda t: kernel_ref[:, CH * t : CH * (t + 1)]
    slope, z_grad, _, score = critic_forward(images_ref[...], lift_half, kernel_of, head_ref[...], patch_ref)
    pre_grad = lift_pullback(slope, z_grad.astype(bf16), kernel_of)
    pull = (-8.0 * dot(lift_half, pre_grad, NT)[:, :FAKE]).astype(bf16)
    for j in range(8):
        copies_ref[j] = pull
    high = score.astype(bf16)
    middle = (score - high.astype(f32)).astype(bf16)
    low = (score - high.astype(f32) - middle.astype(f32)).astype(bf16)
    lane = lax.broadcasted_iota(jnp.int32, (C, 128), 1)
    three = jnp.where(lane == 0, high.astype(f32), jnp.where(lane == 1, middle.astype(f32), jnp.where(lane == 2, low.astype(f32), 0.0)))
    score_ref[...] = three.astype(bf16)


def moved_first_kernel(part_a, part_b, lift_out, kernel_out, head_out, patch_ref, half_ref):
    for t in range(TAPS):
        cols = slice(CH * t, CH * (t + 1))
        half_ref[t, :PART_A] = part_a[:, cols]
        half_ref[t, PART_A:] = part_b[:, cols]
    images = moved_images(part_b, 0)
    lift_half = part_b[2 * C :, KW + 128 : KW + 384]
    lane = part_b[2 * C :, KW + 384 :].astype(f32)
    head = jnp.concatenate([lane[:1], lane[16:17]], axis=1)
    kernel_of = lambda t: half_ref[t]
    slope, z_grad, head_grad, _ = critic_forward(images, lift_half, kernel_of, head, patch_ref)
    pre_grad = lift_pullback(slope, z_grad.astype(bf16), kernel_of)
    lift_out[...] = lift_half.astype(f32) - critic_rate * dot(images[:, :ROWS], pre_grad)
    head_out[...] = head - critic_rate * head_grad
    z_turned = jnp.transpose(z_grad).astype(bf16)
    for t in range(TAPS):
        kernel_out[:, CH * t : CH * (t + 1)] = kernel_of(t).astype(f32) - critic_rate * dot(z_turned, patch_ref[t])


def moved_second_kernel(part_b, lift_ref, kernel_ref, head_ref, lift_out, kernel_out, head_out, patch_ref, half_ref):
    for t in range(TAPS):
        half_ref[t] = kernel_ref[:, CH * t : CH * (t + 1)].astype(bf16)
    lift = lift_ref[...]
    head = head_ref[...]
    images = moved_images(part_b, 1)
    kernel_of = lambda t: half_ref[t]
    slope, z_grad, head_grad, _ = critic_forward(images, lift.astype(bf16), kernel_of, head, patch_ref)
    pre_grad = lift_pullback(slope, z_grad.astype(bf16), kernel_of)
    lift_out[...] = lift - critic_rate * dot(images[:, :ROWS], pre_grad)
    head_out[...] = head - critic_rate * head_grad
    z_turned = jnp.transpose(z_grad).astype(bf16)
    for t in range(TAPS):
        cols = slice(CH * t, CH * (t + 1))
        kernel_out[:, cols] = kernel_ref[:, cols] - critic_rate * dot(z_turned, patch_ref[t])


def generator_step(total, latents, first, second):
    inner = exact_dot(latents, first, NT)
    gate = sigmoid(inner)
    second_grad = exact_dot(total, inner * gate)
    inner_grad = exact_dot(jnp.transpose(total), second) * (gate * (1.0 + inner * (1.0 - gate)))
    first_grad = exact_dot(jnp.transpose(inner_grad), latents)
    return first - generator_rate * first_grad, second - generator_rate * second_grad


def middle_kernel(pick_ref, own_ref, other_ref, noise_ref, first_ref, second_ref, pool_ref, images_ref, first_out, second_out):
    first, second = generator_step(own_ref[...].astype(f32) + other_ref[...].astype(f32), latents_of(noise_ref, 0), first_ref[...], second_ref[...])
    first_out[...] = first
    second_out[...] = second
    inner = exact_dot(latents_of(noise_ref, 1), first, NT)
    fakes = exact_dot(second, inner * sigmoid(inner), NT)
    put_images(images_ref, fakes, real_image(pool_ref, pick_ref, 1))


def last_kernel(place_ref, own_ref, other_ref, noise_ref, first_ref, second_ref, score_ref, first_out, second_out, own_out, scores_out):
    total = own_ref[:, :FAKE].astype(f32) + other_ref[:, :FAKE].astype(f32)
    first, second = generator_step(total, latents_of(noise_ref, 1), first_ref[...], second_ref[...])
    first_out[...] = first
    second_out[...] = second
    own = jnp.zeros((C, C), f32)
    for j in range(N_GRP):
        own = own + jnp.where(place_ref[0] == j, total[:, C * j : C * (j + 1)], 0.0)
    own_out[...] = own
    scores_out[0, 0] = jnp.max(score_ref[...])
    scores_out[1, 0] = jnp.sum(own_ref[:, FAKE:].astype(f32)[:1])


def vmem(*_):
    return pl.BlockSpec(memory_space=pltpu.VMEM)


def smem():
    return pl.BlockSpec(memory_space=pltpu.SMEM)


def call(kernel, name, outs, ins, scratch=(), scalars=0, work=0):
    return pl.pallas_call(
        kernel,
        name=name,
        out_shape=[jax.ShapeDtypeStruct(s, d) for s, d in outs],
        in_specs=[smem()] * scalars + [vmem()] * (len(ins) - scalars),
        out_specs=[vmem()] * len(outs),
        scratch_shapes=list(scratch),
        cost_estimate=pl.CostEstimate(flops=work, bytes_accessed=0, transcendentals=0) if work else None,
        compiler_params=pltpu.CompilerParams(vmem_limit_bytes=24 * 1024 * 1024),
    )(*ins)


def shifted(value, steps):
    count = lax.axis_size("loop")
    return lax.ppermute(value, "loop", [(s, (s + steps) % count) for s in range(count)])


def across(value):
    return lax.ppermute(value, "grp", [(m, m ^ 8) for m in range(N_GRP)])


def swap(copies):
    count = lax.axis_size("loop")
    groups = [[8 * i + j for j in range(8)] for i in range(2 * count)]
    return lax.all_to_all(copies, ("loop", "grp"), 0, 0, axis_index_groups=groups)


def together(*values):
    return lax.optimization_barrier(values)


PATCHES = pltpu.VMEM((TAPS, ROWS, CH), bf16)
HALVES = pltpu.VMEM((TAPS, CH, CH), bf16)


def per_device(real_pool, real_pick, noise_latents, generator_in, generator_out, critic_lift, critic_kernel, critic_head):
    pool = real_pool[0, 0]
    pick = real_pick[0, 0, :, 0]
    first, second = generator_in[0], generator_out[0]
    lift = jnp.swapaxes(critic_lift[0, 0], 0, 1)
    kernel = critic_kernel[0, 0]
    head = critic_head[0, 0][None]

    place = lax.axis_index("grp").astype(jnp.int32)[None]
    own_noise = jnp.swapaxes(noise_latents[0], 1, 2).reshape(ROUNDS * C, 128)
    other_noise = across(own_noise)
    small = (first, second, pool, lift, head, own_noise)
    whole = lambda x: pl.BlockSpec(x.shape, lambda i: (0,) * x.ndim)
    part_a, first, second, pool, lift, head, own_noise = pl.pallas_call(
        stage_kernel,
        name="stage",
        grid=(PART_A // 32,),
        out_shape=[jax.ShapeDtypeStruct((PART_A, KW), bf16)] + [jax.ShapeDtypeStruct(x.shape, x.dtype) for x in small],
        in_specs=[pl.BlockSpec((32, KW), lambda i: (i, 0))] + [whole(x) for x in small],
        out_specs=[pl.BlockSpec((32, KW), lambda i: (i, 0))] + [whole(x) for x in small],
        compiler_params=pltpu.CompilerParams(vmem_limit_bytes=24 * 1024 * 1024),
    )(kernel, *small)
    (copies,) = call(
        noise_copies_kernel, "noise_copies", [((8, 4 * C, 128), bf16)], (place, own_noise, other_noise), scalars=1, work=COPY_WORK
    )
    moved_a = shifted(part_a, 2)
    noise = swap(copies)
    (images,) = call(
        generate_kernel, "make_fakes", [((C, WIDE), bf16)], (pick, noise, first, second, pool), scalars=1
    )
    copies, lift_1, kernel_1, head_1, score_0, part_b = call(
        first_step_kernel,
        "first_step",
        [((8, C, FAKE), bf16), ((C, CH), f32), ((CH, KW), bf16), ((1, CH), f32), ((8, 128), f32), ((PART_B, KW + EXTRA), bf16)],
        (images, lift, kernel, head),
        (PATCHES, HALVES),
        work=FIRST_WORK,
    )
    (partial,) = call(sum_kernel, "sum_first", [((C, FAKE), bf16)], (swap(copies),))
    partial, moved_a = together(partial, moved_a)
    other = across(partial)
    own_images, first_1, second_1 = call(
        middle_kernel,
        "generator_step",
        [((C, WIDE), bf16), ((CH, 128), f32), ((C, CH), f32)],
        (pick, partial, other, noise, first, second, pool),
        scalars=1,
    )
    ahead_images = shifted(own_images, -1)
    (part_b,) = call(
        add_images_kernel, "add_images", [((PART_B, KW + EXTRA), bf16)], (ahead_images, part_b)
    )
    part_b, ahead_images = together(part_b, ahead_images)
    moved_b = shifted(part_b, 2)
    copies, score_1 = call(
        pull_only_kernel,
        "second_pull",
        [((8, C, FAKE), bf16), ((C, 128), bf16)],
        (ahead_images, lift_1, kernel_1, head_1),
        (PATCHES,),
    )
    (partial,) = call(scored_sum_kernel, "sum_second", [((C, WIDE), bf16)], (swap(copies), score_1))
    partial, moved_b = together(partial, moved_b)
    same = shifted(partial, 1)

    moved_lift, moved_kernel, moved_head = call(
        moved_first_kernel,
        "moved_first",
        [((C, CH), f32), ((CH, KW), f32), ((1, CH), f32)],
        (moved_a, moved_b),
        (PATCHES, HALVES),
    )
    moved_lift, same = together(moved_lift, same)
    cross = across(same)
    lift_2, kernel_2, head_2 = call(
        moved_second_kernel,
        "moved_second",
        [((C, CH), f32), ((CH, KW), f32), ((1, CH), f32)],
        (moved_b, moved_lift, moved_kernel, moved_head),
        (PATCHES, HALVES),
    )
    first_2, second_2, own_grad, scores = pl.pallas_call(
        last_kernel,
        name="generator_last",
        out_shape=[
            jax.ShapeDtypeStruct((CH, 128), f32),
            jax.ShapeDtypeStruct((C, CH), f32),
            jax.ShapeDtypeStruct((C, C), f32),
            jax.ShapeDtypeStruct((ROUNDS, 1), f32),
        ],
        in_specs=[smem()] + [vmem()] * 6,
        out_specs=[vmem()] * 3 + [smem()],
        compiler_params=pltpu.CompilerParams(vmem_limit_bytes=24 * 1024 * 1024),
    )(place, same, cross, noise, first_1, second_1, score_0)
    return (
        jnp.swapaxes(lift_2, 0, 1)[None, None],
        kernel_2[None, None],
        head_2.reshape(1, 1, CH),
        first_2[None],
        second_2[None],
        own_grad[None],
        scores[None, None],
    )


def solution(mesh):
    return jax.shard_map(
        per_device,
        mesh=mesh,
        in_specs=(
            P("loop", "grp", None, None, None),
            P("loop", "grp", None, None),
            P("loop", None, None, "grp"),
            P("loop", None, None),
            P("loop", None, None),
            P("loop", "grp", None, None),
            P("loop", "grp", None, None),
            P("loop", "grp", None),
        ),
        out_specs=(
            P("loop", "grp", None, None),
            P("loop", "grp", None, None),
            P("loop", "grp", None),
            P("loop", None, None),
            P("loop", None, None),
            P("loop", None, "grp"),
            P("loop", "grp", None, None),
        ),
        check_vma=False,
    )
```

```python
import functools

import jax
import jax.numpy as jnp
from jax import lax
from jax.experimental import pallas as pl
from jax.experimental.pallas import tpu as pltpu
from jax.sharding import PartitionSpec as P

ROUNDS = 2
CELLS = 64
C = 32
CH = 256
TAPS = 9
N_GRP = 16
FAKE = 512
ROWS = 576
WIDE = 640
KW = TAPS * CH
PART_A = 160
PART_B = CH - PART_A
EXTRA = 512
FIRST_WORK = 2_000_000_000
COPY_WORK = 4_000_000_000

critic_rate = 0.05
generator_rate = 0.2

bf16 = jnp.bfloat16
f32 = jnp.float32
NN = (((1,), (0,)), ((), ()))
NT = (((1,), (1,)), ((), ()))


def dot(a, b, dims=NN):
    return lax.dot_general(a, b, dims, preferred_element_type=f32)


def split(x):
    high = x.astype(bf16)
    return high, (x - high.astype(f32)).astype(bf16)


def exact_dot(a, b, dims=NN):
    if b.dtype == bf16:
        high, low = split(a)
        return dot(high, b, dims) + dot(low, b, dims)
    if a.dtype == bf16:
        high, low = split(b)
        return dot(a, high, dims) + dot(a, low, dims)
    a_high, a_low = split(a)
    b_high, b_low = split(b)
    return dot(a_high, b_high, dims) + (dot(a_high, b_low, dims) + dot(a_low, b_high, dims))


def sigmoid(x):
    return 1.0 / (1.0 + jnp.exp(-x))


def row_ids(width):
    return lax.broadcasted_iota(jnp.int32, (ROWS, width), 0)


def move_rows(x, by):
    if by == 0:
        return x
    pad = jnp.zeros((abs(by), x.shape[1]), x.dtype)
    if by > 0:
        return jnp.concatenate([x[by:], pad], axis=0)
    return jnp.concatenate([pad, x[:by]], axis=0)


def masks():
    rows = row_ids(CH)
    col = rows & 7
    row = (rows >> 3) & 7
    reads_x = {-1: col > 0, 1: col < 7}
    reads_y = {-1: row > 0, 1: row < 7}
    return reads_x, reads_y


def critic_forward(images, lift_t, kernel_of, head, patch_ref):
    reads_x, reads_y = masks()
    images_t = jnp.transpose(images.astype(f32))[:ROWS].astype(bf16)
    pre = dot(images_t, lift_t)
    gate = sigmoid(pre)
    lifted = (pre * gate).astype(bf16).astype(f32)
    slope = gate * (1.0 + pre * (1.0 - gate))
    z = None
    for b in range(3):
        dx = b - 1
        across = lifted
        if dx:
            across = jnp.where(reads_x[dx], pltpu.roll(lifted, (-dx) % ROWS, 0), 0.0)
        for a in range(3):
            dy = a - 1
            tap = move_rows(across, 8 * dy)
            if dy:
                tap = jnp.where(reads_y[dy], tap, 0.0)
            tap = tap.astype(bf16)
            patch_ref[3 * a + b] = tap
            part = dot(tap, kernel_of(3 * a + b), NT)
            z = part if z is None else z + part
    gate = sigmoid(z)
    hidden = z * gate
    weight = jnp.where(row_ids(CH) < FAKE, 1.0 / 64.0, -1.0 / 8.0)
    real_score = jnp.sum(hidden[FAKE:] * head, keepdims=True) / 8.0
    head_grad = jnp.sum(weight * hidden, axis=0, keepdims=True)
    z_grad = (weight * head) * (gate * (1.0 + z * (1.0 - gate)))
    return slope, z_grad, head_grad, real_score


def lift_pullback(slope, z_grad, kernel_of):
    reads_x, reads_y = masks()
    total = None
    for b in range(3):
        dx = b - 1
        across = None
        for a in range(3):
            dy = a - 1
            tap = dot(z_grad, kernel_of(3 * a + b))
            if dy:
                tap = jnp.where(reads_y[dy], tap, 0.0)
            tap = move_rows(tap, -8 * dy)
            across = tap if across is None else across + tap
        if dx:
            across = pltpu.roll(jnp.where(reads_x[dx], across, 0.0), dx % ROWS, 0)
        total = across if total is None else total + across
    return (total * slope).astype(bf16)


def real_image(pool_ref, pick_ref, round_index):
    return pool_ref[pick_ref[round_index]]


def latents_of(noise_ref, round_index):
    halves = []
    for z in range(2):
        start = 2 * C * z + C * round_index
        halves.append(noise_ref[:, start : start + C, :].reshape(FAKE // 2, 128))
    return jnp.concatenate(halves, axis=0)


def put_images(images_ref, fakes, real):
    images_ref[:, :FAKE] = fakes.astype(bf16)
    images_ref[:, FAKE:] = jnp.concatenate([real, jnp.zeros_like(real)], axis=1)


def stage_kernel(*refs):
    count = 6
    kernel_ref, small = refs[0], refs[1 : 1 + count]
    part_ref, small_out = refs[1 + count], refs[2 + count : 2 + 2 * count]
    rows_ref, sems = refs[-2:]
    copies = [pltpu.make_async_copy(kernel_ref.at[:PART_A], rows_ref, sems.at[count])]
    copies += [pltpu.make_async_copy(small[k], small_out[k], sems.at[k]) for k in range(count)]
    for copy in copies:
        copy.start()
    copies[0].wait()
    part_ref[...] = rows_ref[...].astype(bf16)
    for copy in copies[1:]:
        copy.wait()


def noise_copies_kernel(place_ref, own_ref, other_ref, copies_ref):
    own_first = place_ref[0] < 8
    own = own_ref[...].astype(f32)
    other = other_ref[...].astype(f32)
    low = jnp.where(own_first, own, other).astype(bf16)
    high = jnp.where(own_first, other, own).astype(bf16)
    for j in range(8):
        copies_ref[j, : 2 * C] = low
        copies_ref[j, 2 * C :] = high


def sum_of(pulls_ref):
    total = pulls_ref[0].astype(f32)
    for j in range(1, 8):
        total = total + pulls_ref[j].astype(f32)
    return total


def sum_kernel(pulls_ref, out_ref):
    out_ref[...] = sum_of(pulls_ref).astype(bf16)


def scored_sum_kernel(pulls_ref, score_ref, out_ref):
    out_ref[:, :FAKE] = sum_of(pulls_ref).astype(bf16)
    out_ref[:, FAKE:] = score_ref[...]


def add_images_kernel(images_ref, part_in, part_ref):
    part_ref[:, : KW + EXTRA] = part_in[...]
    images = images_ref[...]
    part_ref[C : 2 * C, KW:] = images[:, :FAKE]
    tails = jnp.concatenate([part_in[2 * C :, KW : KW + CELLS], images[:, FAKE : FAKE + CELLS]], axis=1)
    part_ref[2 * C :, KW : KW + 128] = tails


def moved_images(part_ref, which):
    start = CELLS * which
    tails = part_ref[2 * C : 3 * C, KW : KW + 128][:, start : start + CELLS]
    return jnp.concatenate([part_ref[C * which : C * (which + 1), KW:], tails, jnp.zeros_like(tails)], axis=1)


def generate_kernel(pick_ref, noise_ref, first_ref, second_ref, pool_ref, images_ref):
    latents = latents_of(noise_ref, 0)
    inner = exact_dot(latents, first_ref[...], NT)
    fakes = exact_dot(second_ref[...], inner * sigmoid(inner), NT)
    put_images(images_ref, fakes, real_image(pool_ref, pick_ref, 0))


def first_step_kernel(images_ref, lift_ref, kernel_ref, head_ref, copies_ref, lift_out, kernel_out, head_out, score_out, rest_out, patch_ref, half_ref):
    for t in range(TAPS):
        half_ref[t] = kernel_ref[:, CH * t : CH * (t + 1)].astype(bf16)
    lift = lift_ref[...]
    head = head_ref[...]
    lift_half = lift.astype(bf16)
    images = images_ref[...]
    slope, z_grad, head_grad, score = critic_forward(images, lift_half, lambda t: half_ref[t], head, patch_ref)
    z_half = z_grad.astype(bf16)
    pre_grad = lift_pullback(slope, z_half, lambda t: half_ref[t])
    pull = (-8.0 * dot(lift_half, pre_grad, NT)[:, :FAKE]).astype(bf16)
    for j in range(8):
        copies_ref[j] = pull
    lift_out[...] = lift - critic_rate * dot(images[:, :ROWS], pre_grad)
    head_out[...] = head - critic_rate * head_grad
    z_turned = jnp.transpose(z_grad).astype(bf16)
    for t in range(TAPS):
        cols = slice(CH * t, CH * (t + 1))
        kernel_out[:, cols] = (kernel_ref[:, cols] - critic_rate * dot(z_turned, patch_ref[t])).astype(bf16)
        rest_out[:, cols] = half_ref[t, PART_A:, :]
    rest_out[:C, KW:] = images[:, :FAKE]
    rest_out[C : 2 * C, KW:] = jnp.zeros((C, EXTRA), bf16)
    rest_out[2 * C :, KW : KW + 128] = images[:, FAKE:]
    rest_out[2 * C :, KW + 128 : KW + 384] = lift_half
    lane = jnp.concatenate([jnp.broadcast_to(head[:, :128], (16, 128)), jnp.broadcast_to(head[:, 128:], (16, 128))], axis=0)
    rest_out[2 * C :, KW + 384 :] = lane.astype(bf16)
    score_out[...] = jnp.broadcast_to(score, (8, 128))


def pull_only_kernel(images_ref, lift_ref, kernel_ref, head_ref, copies_ref, score_ref, patch_ref):
    lift_half = lift_ref[...].astype(bf16)
    kernel_of = lambda t: kernel_ref[:, CH * t : CH * (t + 1)]
    slope, z_grad, _, score = critic_forward(images_ref[...], lift_half, kernel_of, head_ref[...], patch_ref)
    pre_grad = lift_pullback(slope, z_grad.astype(bf16), kernel_of)
    pull = (-8.0 * dot(lift_half, pre_grad, NT)[:, :FAKE]).astype(bf16)
    for j in range(8):
        copies_ref[j] = pull
    high = score.astype(bf16)
    middle = (score - high.astype(f32)).astype(bf16)
    low = (score - high.astype(f32) - middle.astype(f32)).astype(bf16)
    lane = lax.broadcasted_iota(jnp.int32, (C, 128), 1)
    three = jnp.where(lane == 0, high.astype(f32), jnp.where(lane == 1, middle.astype(f32), jnp.where(lane == 2, low.astype(f32), 0.0)))
    score_ref[...] = three.astype(bf16)


def moved_first_kernel(part_a, part_b, lift_out, kernel_out, head_out, patch_ref, half_ref):
    for t in range(TAPS):
        cols = slice(CH * t, CH * (t + 1))
        half_ref[t, :PART_A] = part_a[:, cols]
        half_ref[t, PART_A:] = part_b[:, cols]
    images = moved_images(part_b, 0)
    lift_half = part_b[2 * C :, KW + 128 : KW + 384]
    lane = part_b[2 * C :, KW + 384 :].astype(f32)
    head = jnp.concatenate([lane[:1], lane[16:17]], axis=1)
    kernel_of = lambda t: half_ref[t]
    slope, z_grad, head_grad, _ = critic_forward(images, lift_half, kernel_of, head, patch_ref)
    pre_grad = lift_pullback(slope, z_grad.astype(bf16), kernel_of)
    lift_out[...] = lift_half.astype(f32) - critic_rate * dot(images[:, :ROWS], pre_grad)
    head_out[...] = head - critic_rate * head_grad
    z_turned = jnp.transpose(z_grad).astype(bf16)
    for t in range(TAPS):
        kernel_out[:, CH * t : CH * (t + 1)] = kernel_of(t).astype(f32) - critic_rate * dot(z_turned, patch_ref[t])


def moved_second_kernel(part_b, lift_ref, kernel_ref, head_ref, lift_out, kernel_out, head_out, patch_ref, half_ref):
    for t in range(TAPS):
        half_ref[t] = kernel_ref[:, CH * t : CH * (t + 1)].astype(bf16)
    lift = lift_ref[...]
    head = head_ref[...]
    images = moved_images(part_b, 1)
    kernel_of = lambda t: half_ref[t]
    slope, z_grad, head_grad, _ = critic_forward(images, lift.astype(bf16), kernel_of, head, patch_ref)
    pre_grad = lift_pullback(slope, z_grad.astype(bf16), kernel_of)
    lift_out[...] = lift - critic_rate * dot(images[:, :ROWS], pre_grad)
    head_out[...] = head - critic_rate * head_grad
    z_turned = jnp.transpose(z_grad).astype(bf16)
    for t in range(TAPS):
        cols = slice(CH * t, CH * (t + 1))
        kernel_out[:, cols] = kernel_ref[:, cols] - critic_rate * dot(z_turned, patch_ref[t])


def generator_step(total, latents, first, second):
    inner = exact_dot(latents, first, NT)
    gate = sigmoid(inner)
    second_grad = exact_dot(total, inner * gate)
    inner_grad = exact_dot(jnp.transpose(total), second) * (gate * (1.0 + inner * (1.0 - gate)))
    first_grad = exact_dot(jnp.transpose(inner_grad), latents)
    return first - generator_rate * first_grad, second - generator_rate * second_grad


def middle_kernel(pick_ref, own_ref, other_ref, noise_ref, first_ref, second_ref, pool_ref, images_ref, first_out, second_out):
    first, second = generator_step(own_ref[...].astype(f32) + other_ref[...].astype(f32), latents_of(noise_ref, 0), first_ref[...], second_ref[...])
    first_out[...] = first
    second_out[...] = second
    inner = exact_dot(latents_of(noise_ref, 1), first, NT)
    fakes = exact_dot(second, inner * sigmoid(inner), NT)
    put_images(images_ref, fakes, real_image(pool_ref, pick_ref, 1))


def last_kernel(place_ref, own_ref, other_ref, noise_ref, first_ref, second_ref, score_ref, first_out, second_out, own_out, scores_out):
    total = own_ref[:, :FAKE].astype(f32) + other_ref[:, :FAKE].astype(f32)
    first, second = generator_step(total, latents_of(noise_ref, 1), first_ref[...], second_ref[...])
    first_out[...] = first
    second_out[...] = second
    own = jnp.zeros((C, C), f32)
    for j in range(N_GRP):
        own = own + jnp.where(place_ref[0] == j, total[:, C * j : C * (j + 1)], 0.0)
    own_out[...] = own
    scores_out[0, 0] = jnp.max(score_ref[...])
    scores_out[1, 0] = jnp.sum(own_ref[:, FAKE:].astype(f32)[:1])


def vmem(*_):
    return pl.BlockSpec(memory_space=pltpu.VMEM)


def smem():
    return pl.BlockSpec(memory_space=pltpu.SMEM)


def call(kernel, name, outs, ins, scratch=(), scalars=0, work=0):
    return pl.pallas_call(
        kernel,
        name=name,
        out_shape=[jax.ShapeDtypeStruct(s, d) for s, d in outs],
        in_specs=[smem()] * scalars + [vmem()] * (len(ins) - scalars),
        out_specs=[vmem()] * len(outs),
        scratch_shapes=list(scratch),
        cost_estimate=pl.CostEstimate(flops=work, bytes_accessed=0, transcendentals=0) if work else None,
        compiler_params=pltpu.CompilerParams(vmem_limit_bytes=24 * 1024 * 1024),
    )(*ins)


def shifted(value, steps):
    count = lax.axis_size("loop")
    return lax.ppermute(value, "loop", [(s, (s + steps) % count) for s in range(count)])


def across(value):
    return lax.ppermute(value, "grp", [(m, m ^ 8) for m in range(N_GRP)])


def swap(copies):
    count = lax.axis_size("loop")
    groups = [[8 * i + j for j in range(8)] for i in range(2 * count)]
    return lax.all_to_all(copies, ("loop", "grp"), 0, 0, axis_index_groups=groups)


def together(*values):
    return lax.optimization_barrier(values)


PATCHES = pltpu.VMEM((TAPS, ROWS, CH), bf16)
HALVES = pltpu.VMEM((TAPS, CH, CH), bf16)


def per_device(real_pool, real_pick, noise_latents, generator_in, generator_out, critic_lift, critic_kernel, critic_head):
    pool = real_pool[0, 0]
    pick = real_pick[0, 0, :, 0]
    first, second = generator_in[0], generator_out[0]
    lift = jnp.swapaxes(critic_lift[0, 0], 0, 1)
    kernel = critic_kernel[0, 0]
    head = critic_head[0, 0][None]

    place = lax.axis_index("grp").astype(jnp.int32)[None]
    own_noise = jnp.swapaxes(noise_latents[0], 1, 2).reshape(ROUNDS * C, 128)
    other_noise = across(own_noise)
    small = (first, second, pool, lift, head, own_noise)
    part_a, first, second, pool, lift, head, own_noise = pl.pallas_call(
        stage_kernel,
        name="stage",
        out_shape=[jax.ShapeDtypeStruct((PART_A, KW), bf16)] + [jax.ShapeDtypeStruct(x.shape, x.dtype) for x in small],
        in_specs=[pl.BlockSpec(memory_space=pltpu.HBM)] * 7,
        out_specs=[vmem()] * 7,
        scratch_shapes=[pltpu.VMEM((PART_A, KW), f32), pltpu.SemaphoreType.DMA((7,))],
        compiler_params=pltpu.CompilerParams(vmem_limit_bytes=56 * 1024 * 1024),
    )(kernel, *small)
    (copies,) = call(
        noise_copies_kernel, "noise_copies", [((8, 4 * C, 128), bf16)], (place, own_noise, other_noise), scalars=1, work=COPY_WORK
    )
    moved_a = shifted(part_a, 2)
    noise = swap(copies)
    (images,) = call(
        generate_kernel, "make_fakes", [((C, WIDE), bf16)], (pick, noise, first, second, pool), scalars=1
    )
    copies, lift_1, kernel_1, head_1, score_0, part_b = call(
        first_step_kernel,
        "first_step",
        [((8, C, FAKE), bf16), ((C, CH), f32), ((CH, KW), bf16), ((1, CH), f32), ((8, 128), f32), ((PART_B, KW + EXTRA), bf16)],
        (images, lift, kernel, head),
        (PATCHES, HALVES),
        work=FIRST_WORK,
    )
    (partial,) = call(sum_kernel, "sum_first", [((C, FAKE), bf16)], (swap(copies),))
    partial, moved_a = together(partial, moved_a)
    other = across(partial)
    own_images, first_1, second_1 = call(
        middle_kernel,
        "generator_step",
        [((C, WIDE), bf16), ((CH, 128), f32), ((C, CH), f32)],
        (pick, partial, other, noise, first, second, pool),
        scalars=1,
    )
    ahead_images = shifted(own_images, -1)
    (part_b,) = call(
        add_images_kernel, "add_images", [((PART_B, KW + EXTRA), bf16)], (ahead_images, part_b)
    )
    part_b, ahead_images = together(part_b, ahead_images)
    moved_b = shifted(part_b, 2)
    copies, score_1 = call(
        pull_only_kernel,
        "second_pull",
        [((8, C, FAKE), bf16), ((C, 128), bf16)],
        (ahead_images, lift_1, kernel_1, head_1),
        (PATCHES,),
    )
    (partial,) = call(scored_sum_kernel, "sum_second", [((C, WIDE), bf16)], (swap(copies), score_1))
    partial, moved_b = together(partial, moved_b)
    same = shifted(partial, 1)

    moved_lift, moved_kernel, moved_head = call(
        moved_first_kernel,
        "moved_first",
        [((C, CH), f32), ((CH, KW), f32), ((1, CH), f32)],
        (moved_a, moved_b),
        (PATCHES, HALVES),
    )
    moved_lift, same = together(moved_lift, same)
    cross = across(same)
    lift_2, kernel_2, head_2 = call(
        moved_second_kernel,
        "moved_second",
        [((C, CH), f32), ((CH, KW), f32), ((1, CH), f32)],
        (moved_b, moved_lift, moved_kernel, moved_head),
        (PATCHES, HALVES),
    )
    first_2, second_2, own_grad, scores = pl.pallas_call(
        last_kernel,
        name="generator_last",
        out_shape=[
            jax.ShapeDtypeStruct((CH, 128), f32),
            jax.ShapeDtypeStruct((C, CH), f32),
            jax.ShapeDtypeStruct((C, C), f32),
            jax.ShapeDtypeStruct((ROUNDS, 1), f32),
        ],
        in_specs=[smem()] + [vmem()] * 6,
        out_specs=[vmem()] * 3 + [smem()],
        compiler_params=pltpu.CompilerParams(vmem_limit_bytes=24 * 1024 * 1024),
    )(place, same, cross, noise, first_1, second_1, score_0)
    return (
        jnp.swapaxes(lift_2, 0, 1)[None, None],
        kernel_2[None, None],
        head_2.reshape(1, 1, CH),
        first_2[None],
        second_2[None],
        own_grad[None],
        scores[None, None],
    )


def solution(mesh):
    return jax.shard_map(
        per_device,
        mesh=mesh,
        in_specs=(
            P("loop", "grp", None, None, None),
            P("loop", "grp", None, None),
            P("loop", None, None, "grp"),
            P("loop", None, None),
            P("loop", None, None),
            P("loop", "grp", None, None),
            P("loop", "grp", None, None),
            P("loop", "grp", None),
        ),
        out_specs=(
            P("loop", "grp", None, None),
            P("loop", "grp", None, None),
            P("loop", "grp", None),
            P("loop", None, None),
            P("loop", None, None),
            P("loop", None, "grp"),
            P("loop", "grp", None, None),
        ),
        check_vma=False,
    )
```

```python
import functools

import jax
import jax.numpy as jnp
from jax import lax
from jax.experimental import pallas as pl
from jax.experimental.pallas import tpu as pltpu
from jax.sharding import PartitionSpec as P

ROUNDS = 2
CELLS = 64
C = 32
CH = 256
TAPS = 9
N_GRP = 16
FAKE = 512
ROWS = 576
WIDE = 640
KW = TAPS * CH
PART_A = 160
PART_B = CH - PART_A
EXTRA = 512
FIRST_WORK = 2_000_000_000
COPY_WORK = 4_000_000_000

critic_rate = 0.05
generator_rate = 0.2

bf16 = jnp.bfloat16
f32 = jnp.float32
NN = (((1,), (0,)), ((), ()))
NT = (((1,), (1,)), ((), ()))


def dot(a, b, dims=NN):
    return lax.dot_general(a, b, dims, preferred_element_type=f32)


def split(x):
    high = x.astype(bf16)
    return high, (x - high.astype(f32)).astype(bf16)


def exact_dot(a, b, dims=NN):
    if b.dtype == bf16:
        high, low = split(a)
        return dot(high, b, dims) + dot(low, b, dims)
    if a.dtype == bf16:
        high, low = split(b)
        return dot(a, high, dims) + dot(a, low, dims)
    a_high, a_low = split(a)
    b_high, b_low = split(b)
    return dot(a_high, b_high, dims) + (dot(a_high, b_low, dims) + dot(a_low, b_high, dims))


def sigmoid(x):
    return 1.0 / (1.0 + jnp.exp(-x))


def row_ids(width):
    return lax.broadcasted_iota(jnp.int32, (ROWS, width), 0)


def move_rows(x, by):
    if by == 0:
        return x
    pad = jnp.zeros((abs(by), x.shape[1]), x.dtype)
    if by > 0:
        return jnp.concatenate([x[by:], pad], axis=0)
    return jnp.concatenate([pad, x[:by]], axis=0)


def masks():
    rows = row_ids(CH)
    col = rows & 7
    row = (rows >> 3) & 7
    reads_x = {-1: col > 0, 1: col < 7}
    reads_y = {-1: row > 0, 1: row < 7}
    return reads_x, reads_y


def critic_forward(images, lift_t, kernel_of, head, patch_ref):
    reads_x, reads_y = masks()
    images_t = jnp.transpose(images.astype(f32))[:ROWS].astype(bf16)
    pre = dot(images_t, lift_t)
    gate = sigmoid(pre)
    lifted = (pre * gate).astype(bf16).astype(f32)
    slope = gate * (1.0 + pre * (1.0 - gate))
    z = None
    for b in range(3):
        dx = b - 1
        across = lifted
        if dx:
            across = jnp.where(reads_x[dx], pltpu.roll(lifted, (-dx) % ROWS, 0), 0.0)
        for a in range(3):
            dy = a - 1
            tap = move_rows(across, 8 * dy)
            if dy:
                tap = jnp.where(reads_y[dy], tap, 0.0)
            tap = tap.astype(bf16)
            patch_ref[3 * a + b] = tap
            part = dot(tap, kernel_of(3 * a + b), NT)
            z = part if z is None else z + part
    gate = sigmoid(z)
    hidden = z * gate
    weight = jnp.where(row_ids(CH) < FAKE, 1.0 / 64.0, -1.0 / 8.0)
    real_score = jnp.sum(hidden[FAKE:] * head, keepdims=True) / 8.0
    head_grad = jnp.sum(weight * hidden, axis=0, keepdims=True)
    z_grad = (weight * head) * (gate * (1.0 + z * (1.0 - gate)))
    return slope, z_grad, head_grad, real_score


def lift_pullback(slope, z_grad, kernel_of):
    reads_x, reads_y = masks()
    total = None
    for b in range(3):
        dx = b - 1
        across = None
        for a in range(3):
            dy = a - 1
            tap = dot(z_grad, kernel_of(3 * a + b))
            if dy:
                tap = jnp.where(reads_y[dy], tap, 0.0)
            tap = move_rows(tap, -8 * dy)
            across = tap if across is None else across + tap
        if dx:
            across = pltpu.roll(jnp.where(reads_x[dx], across, 0.0), dx % ROWS, 0)
        total = across if total is None else total + across
    return (total * slope).astype(bf16)


def real_image(pool_ref, pick_ref, round_index):
    return pool_ref[pick_ref[round_index]]


def latents_of(noise_ref, round_index):
    halves = []
    for z in range(2):
        start = 2 * C * z + C * round_index
        halves.append(noise_ref[:, start : start + C, :].reshape(FAKE // 2, 128))
    return jnp.concatenate(halves, axis=0)


def put_images(images_ref, fakes, real):
    images_ref[:, :FAKE] = fakes.astype(bf16)
    images_ref[:, FAKE:] = jnp.concatenate([real, jnp.zeros_like(real)], axis=1)


def stage_kernel(*refs):
    count = 6
    kernel_ref, small = refs[0], refs[1 : 1 + count]
    part_ref, small_out = refs[1 + count], refs[2 + count : 2 + 2 * count]
    rows_ref, sems = refs[-2:]
    copies = [pltpu.make_async_copy(kernel_ref.at[:PART_A], rows_ref, sems.at[count])]
    copies += [pltpu.make_async_copy(small[k], small_out[k], sems.at[k]) for k in range(count)]
    for copy in copies:
        copy.start()
    copies[0].wait()
    part_ref[...] = rows_ref[...].astype(bf16)
    for copy in copies[1:]:
        copy.wait()


def noise_copies_kernel(place_ref, own_ref, other_ref, copies_ref):
    own_first = place_ref[0] < 8
    own = own_ref[...].astype(f32)
    other = other_ref[...].astype(f32)
    low = jnp.where(own_first, own, other).astype(bf16)
    high = jnp.where(own_first, other, own).astype(bf16)
    for j in range(8):
        copies_ref[j, : 2 * C] = low
        copies_ref[j, 2 * C :] = high


def sum_of(pulls_ref):
    total = pulls_ref[0].astype(f32)
    for j in range(1, 8):
        total = total + pulls_ref[j].astype(f32)
    return total


def sum_kernel(pulls_ref, out_ref):
    out_ref[...] = sum_of(pulls_ref).astype(bf16)


def scored_sum_kernel(pulls_ref, score_ref, out_ref):
    out_ref[:, :FAKE] = sum_of(pulls_ref).astype(bf16)
    out_ref[:, FAKE:] = score_ref[...]


def add_images_kernel(images_ref, part_in, part_ref):
    part_ref[:, : KW + EXTRA] = part_in[...]
    images = images_ref[...]
    part_ref[C : 2 * C, KW:] = images[:, :FAKE]
    tails = jnp.concatenate([part_in[2 * C :, KW : KW + CELLS], images[:, FAKE : FAKE + CELLS]], axis=1)
    part_ref[2 * C :, KW : KW + 128] = tails


def moved_images(part_ref, which):
    start = CELLS * which
    tails = part_ref[2 * C : 3 * C, KW : KW + 128][:, start : start + CELLS]
    return jnp.concatenate([part_ref[C * which : C * (which + 1), KW:], tails, jnp.zeros_like(tails)], axis=1)


def generate_kernel(pick_ref, noise_ref, first_ref, second_ref, pool_ref, images_ref):
    latents = latents_of(noise_ref, 0)
    inner = exact_dot(latents, first_ref[...], NT)
    fakes = exact_dot(second_ref[...], inner * sigmoid(inner), NT)
    put_images(images_ref, fakes, real_image(pool_ref, pick_ref, 0))


def first_step_kernel(images_ref, lift_ref, kernel_ref, head_ref, copies_ref, lift_out, kernel_out, head_out, score_out, rest_out, patch_ref, half_ref):
    for t in range(TAPS):
        half_ref[t] = kernel_ref[:, CH * t : CH * (t + 1)].astype(bf16)
    lift = lift_ref[...]
    head = head_ref[...]
    lift_half = lift.astype(bf16)
    images = images_ref[...]
    slope, z_grad, head_grad, score = critic_forward(images, lift_half, lambda t: half_ref[t], head, patch_ref)
    z_half = z_grad.astype(bf16)
    pre_grad = lift_pullback(slope, z_half, lambda t: half_ref[t])
    pull = (-8.0 * dot(lift_half, pre_grad, NT)[:, :FAKE]).astype(bf16)
    for j in range(8):
        copies_ref[j] = pull
    lift_out[...] = lift - critic_rate * dot(images[:, :ROWS], pre_grad)
    head_out[...] = head - critic_rate * head_grad
    z_turned = jnp.transpose(z_grad).astype(bf16)
    for t in range(TAPS):
        cols = slice(CH * t, CH * (t + 1))
        kernel_out[:, cols] = (kernel_ref[:, cols] - critic_rate * dot(z_turned, patch_ref[t])).astype(bf16)
        rest_out[:, cols] = half_ref[t, PART_A:, :]
    rest_out[:C, KW:] = images[:, :FAKE]
    rest_out[C : 2 * C, KW:] = jnp.zeros((C, EXTRA), bf16)
    rest_out[2 * C :, KW : KW + 128] = images[:, FAKE:]
    rest_out[2 * C :, KW + 128 : KW + 384] = lift_half
    lane = jnp.concatenate([jnp.broadcast_to(head[:, :128], (16, 128)), jnp.broadcast_to(head[:, 128:], (16, 128))], axis=0)
    rest_out[2 * C :, KW + 384 :] = lane.astype(bf16)
    score_out[...] = jnp.broadcast_to(score, (8, 128))


def pull_only_kernel(images_ref, lift_ref, kernel_ref, head_ref, copies_ref, score_ref, patch_ref):
    lift_half = lift_ref[...].astype(bf16)
    kernel_of = lambda t: kernel_ref[:, CH * t : CH * (t + 1)]
    slope, z_grad, _, score = critic_forward(images_ref[...], lift_half, kernel_of, head_ref[...], patch_ref)
    pre_grad = lift_pullback(slope, z_grad.astype(bf16), kernel_of)
    pull = (-8.0 * dot(lift_half, pre_grad, NT)[:, :FAKE]).astype(bf16)
    for j in range(8):
        copies_ref[j] = pull
    high = score.astype(bf16)
    middle = (score - high.astype(f32)).astype(bf16)
    low = (score - high.astype(f32) - middle.astype(f32)).astype(bf16)
    lane = lax.broadcasted_iota(jnp.int32, (C, 128), 1)
    three = jnp.where(lane == 0, high.astype(f32), jnp.where(lane == 1, middle.astype(f32), jnp.where(lane == 2, low.astype(f32), 0.0)))
    score_ref[...] = three.astype(bf16)


def moved_first_kernel(part_a, part_b, lift_out, kernel_out, head_out, patch_ref, half_ref):
    for t in range(TAPS):
        cols = slice(CH * t, CH * (t + 1))
        half_ref[t, :PART_A] = part_a[:, cols]
        half_ref[t, PART_A:] = part_b[:, cols]
    images = moved_images(part_b, 0)
    lift_half = part_b[2 * C :, KW + 128 : KW + 384]
    lane = part_b[2 * C :, KW + 384 :].astype(f32)
    head = jnp.concatenate([lane[:1], lane[16:17]], axis=1)
    kernel_of = lambda t: half_ref[t]
    slope, z_grad, head_grad, _ = critic_forward(images, lift_half, kernel_of, head, patch_ref)
    pre_grad = lift_pullback(slope, z_grad.astype(bf16), kernel_of)
    lift_out[...] = lift_half.astype(f32) - critic_rate * dot(images[:, :ROWS], pre_grad)
    head_out[...] = head - critic_rate * head_grad
    z_turned = jnp.transpose(z_grad).astype(bf16)
    for t in range(TAPS):
        kernel_out[:, CH * t : CH * (t + 1)] = kernel_of(t).astype(f32) - critic_rate * dot(z_turned, patch_ref[t])


def moved_second_kernel(part_b, lift_ref, kernel_ref, head_ref, lift_out, kernel_out, head_out, patch_ref, half_ref, new_ref, sems):
    for t in range(TAPS):
        half_ref[t] = kernel_ref[:, CH * t : CH * (t + 1)].astype(bf16)
    lift = lift_ref[...]
    head = head_ref[...]
    images = moved_images(part_b, 1)
    kernel_of = lambda t: half_ref[t]
    slope, z_grad, head_grad, _ = critic_forward(images, lift.astype(bf16), kernel_of, head, patch_ref)
    pre_grad = lift_pullback(slope, z_grad.astype(bf16), kernel_of)
    lift_out[...] = lift - critic_rate * dot(images[:, :ROWS], pre_grad)
    head_out[...] = head - critic_rate * head_grad
    z_turned = jnp.transpose(z_grad).astype(bf16)
    copies = []
    for t in range(TAPS):
        cols = slice(CH * t, CH * (t + 1))
        new_ref[t] = kernel_ref[:, cols] - critic_rate * dot(z_turned, patch_ref[t])
        copies.append(pltpu.make_async_copy(new_ref.at[t], kernel_out.at[:, cols], sems.at[t]))
        copies[t].start()
    for copy in copies:
        copy.wait()


def generator_step(total, latents, first, second):
    inner = exact_dot(latents, first, NT)
    gate = sigmoid(inner)
    second_grad = exact_dot(total, inner * gate)
    inner_grad = exact_dot(jnp.transpose(total), second) * (gate * (1.0 + inner * (1.0 - gate)))
    first_grad = exact_dot(jnp.transpose(inner_grad), latents)
    return first - generator_rate * first_grad, second - generator_rate * second_grad


def middle_kernel(pick_ref, own_ref, other_ref, noise_ref, first_ref, second_ref, pool_ref, images_ref, first_out, second_out):
    first, second = generator_step(own_ref[...].astype(f32) + other_ref[...].astype(f32), latents_of(noise_ref, 0), first_ref[...], second_ref[...])
    first_out[...] = first
    second_out[...] = second
    inner = exact_dot(latents_of(noise_ref, 1), first, NT)
    fakes = exact_dot(second, inner * sigmoid(inner), NT)
    put_images(images_ref, fakes, real_image(pool_ref, pick_ref, 1))


def last_kernel(place_ref, own_ref, other_ref, noise_ref, first_ref, second_ref, score_ref, first_out, second_out, own_out, scores_out):
    total = own_ref[:, :FAKE].astype(f32) + other_ref[:, :FAKE].astype(f32)
    first, second = generator_step(total, latents_of(noise_ref, 1), first_ref[...], second_ref[...])
    first_out[...] = first
    second_out[...] = second
    own = jnp.zeros((C, C), f32)
    for j in range(N_GRP):
        own = own + jnp.where(place_ref[0] == j, total[:, C * j : C * (j + 1)], 0.0)
    own_out[...] = own
    scores_out[0, 0] = jnp.max(score_ref[...])
    scores_out[0, 1] = jnp.sum(own_ref[:, FAKE:].astype(f32)[:1])


def vmem(*_):
    return pl.BlockSpec(memory_space=pltpu.VMEM)


def smem():
    return pl.BlockSpec(memory_space=pltpu.SMEM)


def call(kernel, name, outs, ins, scratch=(), scalars=0, work=0):
    return pl.pallas_call(
        kernel,
        name=name,
        out_shape=[jax.ShapeDtypeStruct(s, d) for s, d in outs],
        in_specs=[smem()] * scalars + [vmem()] * (len(ins) - scalars),
        out_specs=[vmem()] * len(outs),
        scratch_shapes=list(scratch),
        cost_estimate=pl.CostEstimate(flops=work, bytes_accessed=0, transcendentals=0) if work else None,
        compiler_params=pltpu.CompilerParams(vmem_limit_bytes=24 * 1024 * 1024),
    )(*ins)


def shifted(value, steps):
    count = lax.axis_size("loop")
    return lax.ppermute(value, "loop", [(s, (s + steps) % count) for s in range(count)])


def across(value):
    return lax.ppermute(value, "grp", [(m, m ^ 8) for m in range(N_GRP)])


def swap(copies):
    count = lax.axis_size("loop")
    groups = [[8 * i + j for j in range(8)] for i in range(2 * count)]
    return lax.all_to_all(copies, ("loop", "grp"), 0, 0, axis_index_groups=groups)


def together(*values):
    return lax.optimization_barrier(values)


PATCHES = pltpu.VMEM((TAPS, ROWS, CH), bf16)
HALVES = pltpu.VMEM((TAPS, CH, CH), bf16)


def per_device(real_pool, real_pick, noise_latents, generator_in, generator_out, critic_lift, critic_kernel, critic_head):
    pool = real_pool[0, 0]
    pick = real_pick[0, 0, :, 0]
    first, second = generator_in[0], generator_out[0]
    lift = jnp.swapaxes(critic_lift[0, 0], 0, 1)
    kernel = critic_kernel[0, 0]
    head = critic_head[0, 0][None]

    place = lax.axis_index("grp").astype(jnp.int32)[None]
    own_noise = jnp.swapaxes(noise_latents[0], 1, 2).reshape(ROUNDS * C, 128)
    other_noise = across(own_noise)
    small = (first, second, pool, lift, head, own_noise)
    part_a, first, second, pool, lift, head, own_noise = pl.pallas_call(
        stage_kernel,
        name="stage",
        out_shape=[jax.ShapeDtypeStruct((PART_A, KW), bf16)] + [jax.ShapeDtypeStruct(x.shape, x.dtype) for x in small],
        in_specs=[pl.BlockSpec(memory_space=pltpu.HBM)] * 7,
        out_specs=[vmem()] * 7,
        scratch_shapes=[pltpu.VMEM((PART_A, KW), f32), pltpu.SemaphoreType.DMA((7,))],
        compiler_params=pltpu.CompilerParams(vmem_limit_bytes=56 * 1024 * 1024),
    )(kernel, *small)
    (copies,) = call(
        noise_copies_kernel, "noise_copies", [((8, 4 * C, 128), bf16)], (place, own_noise, other_noise), scalars=1, work=COPY_WORK
    )
    moved_a = shifted(part_a, 2)
    noise = swap(copies)
    (images,) = call(
        generate_kernel, "make_fakes", [((C, WIDE), bf16)], (pick, noise, first, second, pool), scalars=1
    )
    copies, lift_1, kernel_1, head_1, score_0, part_b = call(
        first_step_kernel,
        "first_step",
        [((8, C, FAKE), bf16), ((C, CH), f32), ((CH, KW), bf16), ((1, CH), f32), ((8, 128), f32), ((PART_B, KW + EXTRA), bf16)],
        (images, lift, kernel, head),
        (PATCHES, HALVES),
        work=FIRST_WORK,
    )
    (partial,) = call(sum_kernel, "sum_first", [((C, FAKE), bf16)], (swap(copies),))
    other = across(partial)
    other, moved_a = together(other, moved_a)
    own_images, first_1, second_1 = call(
        middle_kernel,
        "generator_step",
        [((C, WIDE), bf16), ((CH, 128), f32), ((C, CH), f32)],
        (pick, partial, other, noise, first, second, pool),
        scalars=1,
    )
    ahead_images = shifted(own_images, -1)
    (part_b,) = call(
        add_images_kernel, "add_images", [((PART_B, KW + EXTRA), bf16)], (ahead_images, part_b)
    )
    part_b, ahead_images = together(part_b, ahead_images)
    moved_b = shifted(part_b, 2)
    copies, score_1 = call(
        pull_only_kernel,
        "second_pull",
        [((8, C, FAKE), bf16), ((C, 128), bf16)],
        (ahead_images, lift_1, kernel_1, head_1),
        (PATCHES,),
    )
    (partial,) = call(scored_sum_kernel, "sum_second", [((C, WIDE), bf16)], (swap(copies), score_1))
    same = shifted(partial, 1)

    moved_lift, moved_kernel, moved_head = call(
        moved_first_kernel,
        "moved_first",
        [((C, CH), f32), ((CH, KW), f32), ((1, CH), f32)],
        (moved_a, moved_b),
        (PATCHES, HALVES),
    )
    moved_lift, same = together(moved_lift, same)
    cross = across(same)
    lift_2, kernel_2, head_2 = pl.pallas_call(
        moved_second_kernel,
        name="moved_second",
        out_shape=[jax.ShapeDtypeStruct(x, f32) for x in ((C, CH), (CH, KW), (1, CH))],
        in_specs=[vmem()] * 4,
        out_specs=[vmem(), pl.BlockSpec(memory_space=pltpu.HBM), vmem()],
        scratch_shapes=[PATCHES, HALVES, pltpu.VMEM((TAPS, CH, CH), f32), pltpu.SemaphoreType.DMA((TAPS,))],
        compiler_params=pltpu.CompilerParams(vmem_limit_bytes=24 * 1024 * 1024),
    )(moved_b, moved_lift, moved_kernel, moved_head)
    first_2, second_2, own_grad, scores = pl.pallas_call(
        last_kernel,
        name="generator_last",
        out_shape=[
            jax.ShapeDtypeStruct((CH, 128), f32),
            jax.ShapeDtypeStruct((C, CH), f32),
            jax.ShapeDtypeStruct((C, C), f32),
            jax.ShapeDtypeStruct((1, ROUNDS), f32),
        ],
        in_specs=[smem()] + [vmem()] * 6,
        out_specs=[vmem()] * 3 + [smem()],
        compiler_params=pltpu.CompilerParams(vmem_limit_bytes=24 * 1024 * 1024),
    )(place, same, cross, noise, first_1, second_1, score_0)
    return (
        jnp.swapaxes(lift_2, 0, 1)[None, None],
        kernel_2[None, None],
        head_2.reshape(1, 1, CH),
        first_2[None],
        second_2[None],
        own_grad[None],
        scores.reshape(1, 1, ROUNDS, 1),
    )


def solution(mesh):
    return jax.shard_map(
        per_device,
        mesh=mesh,
        in_specs=(
            P("loop", "grp", None, None, None),
            P("loop", "grp", None, None),
            P("loop", None, None, "grp"),
            P("loop", None, None),
            P("loop", None, None),
            P("loop", "grp", None, None),
            P("loop", "grp", None, None),
            P("loop", "grp", None),
        ),
        out_specs=(
            P("loop", "grp", None, None),
            P("loop", "grp", None, None),
            P("loop", "grp", None),
            P("loop", None, None),
            P("loop", None, None),
            P("loop", None, "grp"),
            P("loop", "grp", None, None),
        ),
        check_vma=False,
    )
```

```python
import functools

import jax
import jax.numpy as jnp
from jax import lax
from jax.experimental import pallas as pl
from jax.experimental.pallas import tpu as pltpu
from jax.sharding import PartitionSpec as P

ROUNDS = 2
CELLS = 64
C = 32
CH = 256
TAPS = 9
N_GRP = 16
FAKE = 512
ROWS = 576
WIDE = 640
KW = TAPS * CH
PART_A = 160
PART_B = CH - PART_A
EXTRA = 512
FIRST_WORK = 2_000_000_000
COPY_WORK = 4_000_000_000

critic_rate = 0.05
generator_rate = 0.2

bf16 = jnp.bfloat16
f32 = jnp.float32
NN = (((1,), (0,)), ((), ()))
NT = (((1,), (1,)), ((), ()))


def dot(a, b, dims=NN):
    return lax.dot_general(a, b, dims, preferred_element_type=f32)


def split(x):
    high = x.astype(bf16)
    return high, (x - high.astype(f32)).astype(bf16)


def exact_dot(a, b, dims=NN):
    if b.dtype == bf16:
        high, low = split(a)
        return dot(high, b, dims) + dot(low, b, dims)
    if a.dtype == bf16:
        high, low = split(b)
        return dot(a, high, dims) + dot(a, low, dims)
    a_high, a_low = split(a)
    b_high, b_low = split(b)
    return dot(a_high, b_high, dims) + (dot(a_high, b_low, dims) + dot(a_low, b_high, dims))


def sigmoid(x):
    return 1.0 / (1.0 + jnp.exp(-x))


def row_ids(width):
    return lax.broadcasted_iota(jnp.int32, (ROWS, width), 0)


def move_rows(x, by):
    if by == 0:
        return x
    pad = jnp.zeros((abs(by), x.shape[1]), x.dtype)
    if by > 0:
        return jnp.concatenate([x[by:], pad], axis=0)
    return jnp.concatenate([pad, x[:by]], axis=0)


def masks():
    rows = row_ids(CH)
    col = rows & 7
    row = (rows >> 3) & 7
    reads_x = {-1: col > 0, 1: col < 7}
    reads_y = {-1: row > 0, 1: row < 7}
    return reads_x, reads_y


def critic_forward(images, lift_t, kernel_of, head, patch_ref):
    reads_x, reads_y = masks()
    images_t = jnp.transpose(images.astype(f32))[:ROWS].astype(bf16)
    pre = dot(images_t, lift_t)
    gate = sigmoid(pre)
    lifted = (pre * gate).astype(bf16).astype(f32)
    slope = gate * (1.0 + pre * (1.0 - gate))
    for b in range(3):
        dx = b - 1
        side = lifted
        if dx:
            side = jnp.where(reads_x[dx], pltpu.roll(lifted, (-dx) % ROWS, 0), 0.0)
        patch_ref[b] = side.astype(bf16)
    z = None
    for a in (1, 0, 2):
        dy = a - 1
        part = dot(patch_ref[0], kernel_of(3 * a), NT)
        part = part + dot(patch_ref[1], kernel_of(3 * a + 1), NT)
        part = part + dot(patch_ref[2], kernel_of(3 * a + 2), NT)
        if dy:
            part = jnp.where(reads_y[dy], move_rows(part, 8 * dy), 0.0)
        z = part if z is None else z + part
    gate = sigmoid(z)
    hidden = z * gate
    weight = jnp.where(row_ids(CH) < FAKE, 1.0 / 64.0, -1.0 / 8.0)
    real_score = jnp.sum(hidden[FAKE:] * head, keepdims=True) / 8.0
    head_grad = jnp.sum(weight * hidden, axis=0, keepdims=True)
    z_grad = (weight * head) * (gate * (1.0 + z * (1.0 - gate)))
    return slope, z_grad, head_grad, real_score


def row_parts(z_grad):
    _, reads_y = masks()
    parts = []
    for a in range(3):
        dy = a - 1
        part = z_grad
        if dy:
            part = move_rows(jnp.where(reads_y[dy], part, 0.0), -8 * dy)
        parts.append(part)
    return parts


def lift_pullback(slope, parts, kernel_of):
    reads_x, _ = masks()
    halves = [part.astype(bf16) for part in parts]
    total = None
    for b in range(3):
        dx = b - 1
        side = dot(halves[0], kernel_of(b))
        side = side + dot(halves[1], kernel_of(3 + b))
        side = side + dot(halves[2], kernel_of(6 + b))
        if dx:
            side = pltpu.roll(jnp.where(reads_x[dx], side, 0.0), dx % ROWS, 0)
        total = side if total is None else total + side
    return (total * slope).astype(bf16)


def turned(parts):
    return [jnp.transpose(part).astype(bf16) for part in parts]


def real_image(pool_ref, pick_ref, round_index):
    return pool_ref[pick_ref[round_index]]


def latents_of(noise_ref, round_index):
    halves = []
    for z in range(2):
        start = 2 * C * z + C * round_index
        halves.append(noise_ref[:, start : start + C, :].reshape(FAKE // 2, 128))
    return jnp.concatenate(halves, axis=0)


def put_images(images_ref, fakes, real):
    images_ref[:, :FAKE] = fakes.astype(bf16)
    images_ref[:, FAKE:] = jnp.concatenate([real, jnp.zeros_like(real)], axis=1)


def stage_kernel(*refs):
    count = 6
    kernel_ref, small = refs[0], refs[1 : 1 + count]
    part_ref, small_out = refs[1 + count], refs[2 + count : 2 + 2 * count]
    rows_ref, sems = refs[-2:]
    copies = [pltpu.make_async_copy(kernel_ref.at[:PART_A], rows_ref, sems.at[count])]
    copies += [pltpu.make_async_copy(small[k], small_out[k], sems.at[k]) for k in range(count)]
    for copy in copies:
        copy.start()
    copies[0].wait()
    part_ref[...] = rows_ref[...].astype(bf16)
    for copy in copies[1:]:
        copy.wait()


def noise_copies_kernel(place_ref, own_ref, other_ref, copies_ref):
    own_first = place_ref[0] < 8
    own = own_ref[...].astype(f32)
    other = other_ref[...].astype(f32)
    low = jnp.where(own_first, own, other).astype(bf16)
    high = jnp.where(own_first, other, own).astype(bf16)
    for j in range(8):
        copies_ref[j, : 2 * C] = low
        copies_ref[j, 2 * C :] = high


def sum_of(pulls_ref):
    total = pulls_ref[0].astype(f32)
    for j in range(1, 8):
        total = total + pulls_ref[j].astype(f32)
    return total


def sum_kernel(pulls_ref, out_ref):
    out_ref[...] = sum_of(pulls_ref).astype(bf16)


def scored_sum_kernel(pulls_ref, score_ref, out_ref):
    out_ref[:, :FAKE] = sum_of(pulls_ref).astype(bf16)
    out_ref[:, FAKE:] = score_ref[...]


def add_images_kernel(images_ref, part_in, part_ref):
    part_ref[:, : KW + EXTRA] = part_in[...]
    images = images_ref[...]
    part_ref[C : 2 * C, KW:] = images[:, :FAKE]
    tails = jnp.concatenate([part_in[2 * C :, KW : KW + CELLS], images[:, FAKE : FAKE + CELLS]], axis=1)
    part_ref[2 * C :, KW : KW + 128] = tails


def moved_images(part_ref, which):
    start = CELLS * which
    tails = part_ref[2 * C : 3 * C, KW : KW + 128][:, start : start + CELLS]
    return jnp.concatenate([part_ref[C * which : C * (which + 1), KW:], tails, jnp.zeros_like(tails)], axis=1)


def generate_kernel(pick_ref, noise_ref, first_ref, second_ref, pool_ref, images_ref):
    latents = latents_of(noise_ref, 0)
    inner = exact_dot(latents, first_ref[...], NT)
    fakes = exact_dot(second_ref[...], inner * sigmoid(inner), NT)
    put_images(images_ref, fakes, real_image(pool_ref, pick_ref, 0))


def first_step_kernel(images_ref, lift_ref, kernel_ref, head_ref, copies_ref, lift_out, kernel_out, head_out, score_out, rest_out, patch_ref, half_ref):
    for t in range(TAPS):
        half_ref[t] = kernel_ref[:, CH * t : CH * (t + 1)].astype(bf16)
    lift = lift_ref[...]
    head = head_ref[...]
    lift_half = lift.astype(bf16)
    images = images_ref[...]
    slope, z_grad, head_grad, score = critic_forward(images, lift_half, lambda t: half_ref[t], head, patch_ref)
    parts = row_parts(z_grad)
    pre_grad = lift_pullback(slope, parts, lambda t: half_ref[t])
    pull = (-8.0 * dot(lift_half, pre_grad, NT)[:, :FAKE]).astype(bf16)
    for j in range(8):
        copies_ref[j] = pull
    lift_out[...] = lift - critic_rate * dot(images[:, :ROWS], pre_grad)
    head_out[...] = head - critic_rate * head_grad
    z_turned = turned(parts)
    for t in range(TAPS):
        cols = slice(CH * t, CH * (t + 1))
        kernel_out[:, cols] = (kernel_ref[:, cols] - critic_rate * dot(z_turned[t // 3], patch_ref[t % 3])).astype(bf16)
        rest_out[:, cols] = half_ref[t, PART_A:, :]
    rest_out[:C, KW:] = images[:, :FAKE]
    rest_out[C : 2 * C, KW:] = jnp.zeros((C, EXTRA), bf16)
    rest_out[2 * C :, KW : KW + 128] = images[:, FAKE:]
    rest_out[2 * C :, KW + 128 : KW + 384] = lift_half
    lane = jnp.concatenate([jnp.broadcast_to(head[:, :128], (16, 128)), jnp.broadcast_to(head[:, 128:], (16, 128))], axis=0)
    rest_out[2 * C :, KW + 384 :] = lane.astype(bf16)
    score_out[...] = jnp.broadcast_to(score, (8, 128))


def pull_only_kernel(images_ref, lift_ref, kernel_ref, head_ref, copies_ref, score_ref, patch_ref):
    lift_half = lift_ref[...].astype(bf16)
    kernel_of = lambda t: kernel_ref[:, CH * t : CH * (t + 1)]
    slope, z_grad, _, score = critic_forward(images_ref[...], lift_half, kernel_of, head_ref[...], patch_ref)
    parts = row_parts(z_grad)
    pre_grad = lift_pullback(slope, parts, kernel_of)
    pull = (-8.0 * dot(lift_half, pre_grad, NT)[:, :FAKE]).astype(bf16)
    for j in range(8):
        copies_ref[j] = pull
    high = score.astype(bf16)
    middle = (score - high.astype(f32)).astype(bf16)
    low = (score - high.astype(f32) - middle.astype(f32)).astype(bf16)
    lane = lax.broadcasted_iota(jnp.int32, (C, 128), 1)
    three = jnp.where(lane == 0, high.astype(f32), jnp.where(lane == 1, middle.astype(f32), jnp.where(lane == 2, low.astype(f32), 0.0)))
    score_ref[...] = three.astype(bf16)


def moved_first_kernel(part_a, part_b, lift_out, kernel_out, head_out, patch_ref, half_ref):
    for t in range(TAPS):
        cols = slice(CH * t, CH * (t + 1))
        half_ref[t, :PART_A] = part_a[:, cols]
        half_ref[t, PART_A:] = part_b[:, cols]
    images = moved_images(part_b, 0)
    lift_half = part_b[2 * C :, KW + 128 : KW + 384]
    lane = part_b[2 * C :, KW + 384 :].astype(f32)
    head = jnp.concatenate([lane[:1], lane[16:17]], axis=1)
    kernel_of = lambda t: half_ref[t]
    slope, z_grad, head_grad, _ = critic_forward(images, lift_half, kernel_of, head, patch_ref)
    parts = row_parts(z_grad)
    pre_grad = lift_pullback(slope, parts, kernel_of)
    lift_out[...] = lift_half.astype(f32) - critic_rate * dot(images[:, :ROWS], pre_grad)
    head_out[...] = head - critic_rate * head_grad
    z_turned = turned(parts)
    for t in range(TAPS):
        kernel_out[:, CH * t : CH * (t + 1)] = kernel_of(t).astype(f32) - critic_rate * dot(z_turned[t // 3], patch_ref[t % 3])


def moved_second_kernel(part_b, lift_ref, kernel_ref, head_ref, lift_out, kernel_out, head_out, patch_ref, half_ref, new_ref, sems):
    for t in range(TAPS):
        half_ref[t] = kernel_ref[:, CH * t : CH * (t + 1)].astype(bf16)
    lift = lift_ref[...]
    head = head_ref[...]
    images = moved_images(part_b, 1)
    kernel_of = lambda t: half_ref[t]
    slope, z_grad, head_grad, _ = critic_forward(images, lift.astype(bf16), kernel_of, head, patch_ref)
    parts = row_parts(z_grad)
    pre_grad = lift_pullback(slope, parts, kernel_of)
    lift_out[...] = lift - critic_rate * dot(images[:, :ROWS], pre_grad)
    head_out[...] = head - critic_rate * head_grad
    z_turned = turned(parts)
    copies = []
    for t in range(TAPS):
        cols = slice(CH * t, CH * (t + 1))
        new_ref[t] = kernel_ref[:, cols] - critic_rate * dot(z_turned[t // 3], patch_ref[t % 3])
        copies.append(pltpu.make_async_copy(new_ref.at[t], kernel_out.at[:, cols], sems.at[t]))
        copies[t].start()
    for copy in copies:
        copy.wait()


def generator_step(total, latents, first, second):
    inner = exact_dot(latents, first, NT)
    gate = sigmoid(inner)
    second_grad = exact_dot(total, inner * gate)
    inner_grad = exact_dot(jnp.transpose(total), second) * (gate * (1.0 + inner * (1.0 - gate)))
    first_grad = exact_dot(jnp.transpose(inner_grad), latents)
    return first - generator_rate * first_grad, second - generator_rate * second_grad


def middle_kernel(pick_ref, own_ref, other_ref, noise_ref, first_ref, second_ref, pool_ref, images_ref, first_out, second_out):
    first, second = generator_step(own_ref[...].astype(f32) + other_ref[...].astype(f32), latents_of(noise_ref, 0), first_ref[...], second_ref[...])
    first_out[...] = first
    second_out[...] = second
    inner = exact_dot(latents_of(noise_ref, 1), first, NT)
    fakes = exact_dot(second, inner * sigmoid(inner), NT)
    put_images(images_ref, fakes, real_image(pool_ref, pick_ref, 1))


def last_kernel(place_ref, own_ref, other_ref, noise_ref, first_ref, second_ref, score_ref, first_out, second_out, own_out, scores_out):
    total = own_ref[:, :FAKE].astype(f32) + other_ref[:, :FAKE].astype(f32)
    first, second = generator_step(total, latents_of(noise_ref, 1), first_ref[...], second_ref[...])
    first_out[...] = first
    second_out[...] = second
    own = jnp.zeros((C, C), f32)
    for j in range(N_GRP):
        own = own + jnp.where(place_ref[0] == j, total[:, C * j : C * (j + 1)], 0.0)
    own_out[...] = own
    scores_out[0, 0] = jnp.max(score_ref[...])
    scores_out[0, 1] = jnp.sum(own_ref[:, FAKE:].astype(f32)[:1])


def vmem(*_):
    return pl.BlockSpec(memory_space=pltpu.VMEM)


def smem():
    return pl.BlockSpec(memory_space=pltpu.SMEM)


def call(kernel, name, outs, ins, scratch=(), scalars=0, work=0):
    return pl.pallas_call(
        kernel,
        name=name,
        out_shape=[jax.ShapeDtypeStruct(s, d) for s, d in outs],
        in_specs=[smem()] * scalars + [vmem()] * (len(ins) - scalars),
        out_specs=[vmem()] * len(outs),
        scratch_shapes=list(scratch),
        cost_estimate=pl.CostEstimate(flops=work, bytes_accessed=0, transcendentals=0) if work else None,
        compiler_params=pltpu.CompilerParams(vmem_limit_bytes=24 * 1024 * 1024),
    )(*ins)


def shifted(value, steps):
    count = lax.axis_size("loop")
    return lax.ppermute(value, "loop", [(s, (s + steps) % count) for s in range(count)])


def across(value):
    return lax.ppermute(value, "grp", [(m, m ^ 8) for m in range(N_GRP)])


def swap(copies):
    count = lax.axis_size("loop")
    groups = [[8 * i + j for j in range(8)] for i in range(2 * count)]
    return lax.all_to_all(copies, ("loop", "grp"), 0, 0, axis_index_groups=groups)


def together(*values):
    return lax.optimization_barrier(values)


PATCHES = pltpu.VMEM((3, ROWS, CH), bf16)
HALVES = pltpu.VMEM((TAPS, CH, CH), bf16)


def per_device(real_pool, real_pick, noise_latents, generator_in, generator_out, critic_lift, critic_kernel, critic_head):
    pool = real_pool[0, 0]
    pick = real_pick[0, 0, :, 0]
    first, second = generator_in[0], generator_out[0]
    lift = jnp.swapaxes(critic_lift[0, 0], 0, 1)
    kernel = critic_kernel[0, 0]
    head = critic_head[0, 0][None]

    place = lax.axis_index("grp").astype(jnp.int32)[None]
    own_noise = jnp.swapaxes(noise_latents[0], 1, 2).reshape(ROUNDS * C, 128)
    other_noise = across(own_noise)
    small = (first, second, pool, lift, head, own_noise)
    part_a, first, second, pool, lift, head, own_noise = pl.pallas_call(
        stage_kernel,
        name="stage",
        out_shape=[jax.ShapeDtypeStruct((PART_A, KW), bf16)] + [jax.ShapeDtypeStruct(x.shape, x.dtype) for x in small],
        in_specs=[pl.BlockSpec(memory_space=pltpu.HBM)] * 7,
        out_specs=[vmem()] * 7,
        scratch_shapes=[pltpu.VMEM((PART_A, KW), f32), pltpu.SemaphoreType.DMA((7,))],
        compiler_params=pltpu.CompilerParams(vmem_limit_bytes=56 * 1024 * 1024),
    )(kernel, *small)
    (copies,) = call(
        noise_copies_kernel, "noise_copies", [((8, 4 * C, 128), bf16)], (place, own_noise, other_noise), scalars=1, work=COPY_WORK
    )
    moved_a = shifted(part_a, 2)
    noise = swap(copies)
    (images,) = call(
        generate_kernel, "make_fakes", [((C, WIDE), bf16)], (pick, noise, first, second, pool), scalars=1
    )
    copies, lift_1, kernel_1, head_1, score_0, part_b = call(
        first_step_kernel,
        "first_step",
        [((8, C, FAKE), bf16), ((C, CH), f32), ((CH, KW), bf16), ((1, CH), f32), ((8, 128), f32), ((PART_B, KW + EXTRA), bf16)],
        (images, lift, kernel, head),
        (PATCHES, HALVES),
        work=FIRST_WORK,
    )
    (partial,) = call(sum_kernel, "sum_first", [((C, FAKE), bf16)], (swap(copies),))
    other = across(partial)
    other, moved_a = together(other, moved_a)
    own_images, first_1, second_1 = call(
        middle_kernel,
        "generator_step",
        [((C, WIDE), bf16), ((CH, 128), f32), ((C, CH), f32)],
        (pick, partial, other, noise, first, second, pool),
        scalars=1,
    )
    ahead_images = shifted(own_images, -1)
    (part_b,) = call(
        add_images_kernel, "add_images", [((PART_B, KW + EXTRA), bf16)], (ahead_images, part_b)
    )
    part_b, ahead_images = together(part_b, ahead_images)
    moved_b = shifted(part_b, 2)
    copies, score_1 = call(
        pull_only_kernel,
        "second_pull",
        [((8, C, FAKE), bf16), ((C, 128), bf16)],
        (ahead_images, lift_1, kernel_1, head_1),
        (PATCHES,),
    )
    (partial,) = call(scored_sum_kernel, "sum_second", [((C, WIDE), bf16)], (swap(copies), score_1))
    same = shifted(partial, 1)

    moved_lift, moved_kernel, moved_head = call(
        moved_first_kernel,
        "moved_first",
        [((C, CH), f32), ((CH, KW), f32), ((1, CH), f32)],
        (moved_a, moved_b),
        (PATCHES, HALVES),
    )
    moved_lift, same = together(moved_lift, same)
    cross = across(same)
    lift_2, kernel_2, head_2 = pl.pallas_call(
        moved_second_kernel,
        name="moved_second",
        out_shape=[jax.ShapeDtypeStruct(x, f32) for x in ((C, CH), (CH, KW), (1, CH))],
        in_specs=[vmem()] * 4,
        out_specs=[vmem(), pl.BlockSpec(memory_space=pltpu.HBM), vmem()],
        scratch_shapes=[PATCHES, HALVES, pltpu.VMEM((TAPS, CH, CH), f32), pltpu.SemaphoreType.DMA((TAPS,))],
        compiler_params=pltpu.CompilerParams(vmem_limit_bytes=24 * 1024 * 1024),
    )(moved_b, moved_lift, moved_kernel, moved_head)
    first_2, second_2, own_grad, scores = pl.pallas_call(
        last_kernel,
        name="generator_last",
        out_shape=[
            jax.ShapeDtypeStruct((CH, 128), f32),
            jax.ShapeDtypeStruct((C, CH), f32),
            jax.ShapeDtypeStruct((C, C), f32),
            jax.ShapeDtypeStruct((1, ROUNDS), f32),
        ],
        in_specs=[smem()] + [vmem()] * 6,
        out_specs=[vmem()] * 3 + [smem()],
        compiler_params=pltpu.CompilerParams(vmem_limit_bytes=24 * 1024 * 1024),
    )(place, same, cross, noise, first_1, second_1, score_0)
    return (
        jnp.swapaxes(lift_2, 0, 1)[None, None],
        kernel_2[None, None],
        head_2.reshape(1, 1, CH),
        first_2[None],
        second_2[None],
        own_grad[None],
        scores.reshape(1, 1, ROUNDS, 1),
    )


def solution(mesh):
    return jax.shard_map(
        per_device,
        mesh=mesh,
        in_specs=(
            P("loop", "grp", None, None, None),
            P("loop", "grp", None, None),
            P("loop", None, None, "grp"),
            P("loop", None, None),
            P("loop", None, None),
            P("loop", "grp", None, None),
            P("loop", "grp", None, None),
            P("loop", "grp", None),
        ),
        out_specs=(
            P("loop", "grp", None, None),
            P("loop", "grp", None, None),
            P("loop", "grp", None),
            P("loop", None, None),
            P("loop", None, None),
            P("loop", None, "grp"),
            P("loop", "grp", None, None),
        ),
        check_vma=False,
    )
```

```python
import functools

import jax
import jax.numpy as jnp
from jax import lax
from jax.experimental import pallas as pl
from jax.experimental.pallas import tpu as pltpu
from jax.sharding import PartitionSpec as P

ROUNDS = 2
CELLS = 64
C = 32
CH = 256
TAPS = 9
N_GRP = 16
FAKE = 512
ROWS = 576
WIDE = 640
KW = TAPS * CH
PART_A = 160
PART_B = CH - PART_A
EXTRA = 512
FIRST_WORK = 20_000_000_000
COPY_WORK = 1_000_000

critic_rate = 0.05
generator_rate = 0.2

bf16 = jnp.bfloat16
f32 = jnp.float32
NN = (((1,), (0,)), ((), ()))
NT = (((1,), (1,)), ((), ()))


def dot(a, b, dims=NN):
    return lax.dot_general(a, b, dims, preferred_element_type=f32)


def split(x):
    high = x.astype(bf16)
    return high, (x - high.astype(f32)).astype(bf16)


def exact_dot(a, b, dims=NN):
    if b.dtype == bf16:
        high, low = split(a)
        return dot(high, b, dims) + dot(low, b, dims)
    if a.dtype == bf16:
        high, low = split(b)
        return dot(a, high, dims) + dot(a, low, dims)
    a_high, a_low = split(a)
    b_high, b_low = split(b)
    return dot(a_high, b_high, dims) + (dot(a_high, b_low, dims) + dot(a_low, b_high, dims))


def sigmoid(x):
    return 1.0 / (1.0 + jnp.exp(-x))


def row_ids(width):
    return lax.broadcasted_iota(jnp.int32, (ROWS, width), 0)


def move_rows(x, by):
    if by == 0:
        return x
    pad = jnp.zeros((abs(by), x.shape[1]), x.dtype)
    if by > 0:
        return jnp.concatenate([x[by:], pad], axis=0)
    return jnp.concatenate([pad, x[:by]], axis=0)


def masks():
    rows = row_ids(CH)
    col = rows & 7
    row = (rows >> 3) & 7
    reads_x = {-1: col > 0, 1: col < 7}
    reads_y = {-1: row > 0, 1: row < 7}
    return reads_x, reads_y


def critic_forward(images, lift_t, kernel_of, head, patch_ref):
    reads_x, reads_y = masks()
    images_t = jnp.transpose(images.astype(f32))[:ROWS].astype(bf16)
    pre = dot(images_t, lift_t)
    gate = sigmoid(pre)
    lifted = (pre * gate).astype(bf16).astype(f32)
    slope = gate * (1.0 + pre * (1.0 - gate))
    for b in range(3):
        dx = b - 1
        side = lifted
        if dx:
            side = jnp.where(reads_x[dx], pltpu.roll(lifted, (-dx) % ROWS, 0), 0.0)
        patch_ref[b] = side.astype(bf16)
    z = None
    for a in (1, 0, 2):
        dy = a - 1
        part = dot(patch_ref[0], kernel_of(3 * a), NT)
        part = part + dot(patch_ref[1], kernel_of(3 * a + 1), NT)
        part = part + dot(patch_ref[2], kernel_of(3 * a + 2), NT)
        if dy:
            part = jnp.where(reads_y[dy], move_rows(part, 8 * dy), 0.0)
        z = part if z is None else z + part
    gate = sigmoid(z)
    hidden = z * gate
    weight = jnp.where(row_ids(CH) < FAKE, 1.0 / 64.0, -1.0 / 8.0)
    real_score = jnp.sum(hidden[FAKE:] * head, keepdims=True) / 8.0
    head_grad = jnp.sum(weight * hidden, axis=0, keepdims=True)
    z_grad = (weight * head) * (gate * (1.0 + z * (1.0 - gate)))
    return slope, z_grad, head_grad, real_score


def row_parts(z_grad):
    _, reads_y = masks()
    parts = []
    for a in range(3):
        dy = a - 1
        part = z_grad
        if dy:
            part = move_rows(jnp.where(reads_y[dy], part, 0.0), -8 * dy)
        parts.append(part)
    return parts


def lift_pullback(slope, parts, kernel_of):
    reads_x, _ = masks()
    halves = [part.astype(bf16) for part in parts]
    total = None
    for b in range(3):
        dx = b - 1
        side = dot(halves[0], kernel_of(b))
        side = side + dot(halves[1], kernel_of(3 + b))
        side = side + dot(halves[2], kernel_of(6 + b))
        if dx:
            side = pltpu.roll(jnp.where(reads_x[dx], side, 0.0), dx % ROWS, 0)
        total = side if total is None else total + side
    return (total * slope).astype(bf16)


def turned(parts):
    return [jnp.transpose(part).astype(bf16) for part in parts]


def real_image(pool_ref, pick_ref, round_index):
    return pool_ref[pick_ref[round_index]]


def latents_of(noise_ref, round_index):
    halves = []
    for z in range(2):
        start = 2 * C * z + C * round_index
        halves.append(noise_ref[:, start : start + C, :].reshape(FAKE // 2, 128))
    return jnp.concatenate(halves, axis=0)


def put_images(images_ref, fakes, real):
    images_ref[:, :FAKE] = fakes.astype(bf16)
    images_ref[:, FAKE:] = jnp.concatenate([real, jnp.zeros_like(real)], axis=1)


def stage_kernel(*refs):
    count = 6
    kernel_ref, small = refs[0], refs[1 : 1 + count]
    part_ref, small_out = refs[1 + count], refs[2 + count : 2 + 2 * count]
    rows_ref, sems = refs[-2:]
    copies = [pltpu.make_async_copy(kernel_ref.at[:PART_A], rows_ref, sems.at[count])]
    copies += [pltpu.make_async_copy(small[k], small_out[k], sems.at[k]) for k in range(count)]
    for copy in copies:
        copy.start()
    copies[0].wait()
    part_ref[...] = rows_ref[...].astype(bf16)
    for copy in copies[1:]:
        copy.wait()


def noise_copies_kernel(place_ref, own_ref, other_ref, copies_ref):
    own_first = place_ref[0] < 8
    own = own_ref[...].astype(f32)
    other = other_ref[...].astype(f32)
    low = jnp.where(own_first, own, other).astype(bf16)
    high = jnp.where(own_first, other, own).astype(bf16)
    for j in range(8):
        copies_ref[j, : 2 * C] = low
        copies_ref[j, 2 * C :] = high


def sum_of(pulls_ref):
    total = pulls_ref[0].astype(f32)
    for j in range(1, 8):
        total = total + pulls_ref[j].astype(f32)
    return total


def sum_kernel(pulls_ref, out_ref):
    out_ref[...] = sum_of(pulls_ref).astype(bf16)


def scored_sum_kernel(pulls_ref, score_ref, out_ref):
    out_ref[:, :FAKE] = sum_of(pulls_ref).astype(bf16)
    out_ref[:, FAKE:] = score_ref[...]


def add_images_kernel(images_ref, part_in, part_ref):
    part_ref[:, : KW + EXTRA] = part_in[...]
    images = images_ref[...]
    part_ref[C : 2 * C, KW:] = images[:, :FAKE]
    tails = jnp.concatenate([part_in[2 * C :, KW : KW + CELLS], images[:, FAKE : FAKE + CELLS]], axis=1)
    part_ref[2 * C :, KW : KW + 128] = tails


def moved_images(part_ref, which):
    start = CELLS * which
    tails = part_ref[2 * C : 3 * C, KW : KW + 128][:, start : start + CELLS]
    return jnp.concatenate([part_ref[C * which : C * (which + 1), KW:], tails, jnp.zeros_like(tails)], axis=1)


def generate_kernel(pick_ref, noise_ref, first_ref, second_ref, pool_ref, images_ref):
    latents = latents_of(noise_ref, 0)
    inner = exact_dot(latents, first_ref[...], NT)
    fakes = exact_dot(second_ref[...], inner * sigmoid(inner), NT)
    put_images(images_ref, fakes, real_image(pool_ref, pick_ref, 0))


def first_step_kernel(images_ref, lift_ref, kernel_ref, head_ref, copies_ref, lift_out, kernel_out, head_out, score_out, rest_out, patch_ref, half_ref):
    for t in range(TAPS):
        half_ref[t] = kernel_ref[:, CH * t : CH * (t + 1)].astype(bf16)
    lift = lift_ref[...]
    head = head_ref[...]
    lift_half = lift.astype(bf16)
    images = images_ref[...]
    slope, z_grad, head_grad, score = critic_forward(images, lift_half, lambda t: half_ref[t], head, patch_ref)
    parts = row_parts(z_grad)
    pre_grad = lift_pullback(slope, parts, lambda t: half_ref[t])
    pull = (-8.0 * dot(lift_half, pre_grad, NT)[:, :FAKE]).astype(bf16)
    for j in range(8):
        copies_ref[j] = pull
    lift_out[...] = lift - critic_rate * dot(images[:, :ROWS], pre_grad)
    head_out[...] = head - critic_rate * head_grad
    z_turned = turned(parts)
    for t in range(TAPS):
        cols = slice(CH * t, CH * (t + 1))
        kernel_out[:, cols] = (kernel_ref[:, cols] - critic_rate * dot(z_turned[t // 3], patch_ref[t % 3])).astype(bf16)
        rest_out[:, cols] = half_ref[t, PART_A:, :]
    rest_out[:C, KW:] = images[:, :FAKE]
    rest_out[C : 2 * C, KW:] = jnp.zeros((C, EXTRA), bf16)
    rest_out[2 * C :, KW : KW + 128] = images[:, FAKE:]
    rest_out[2 * C :, KW + 128 : KW + 384] = lift_half
    lane = jnp.concatenate([jnp.broadcast_to(head[:, :128], (16, 128)), jnp.broadcast_to(head[:, 128:], (16, 128))], axis=0)
    rest_out[2 * C :, KW + 384 :] = lane.astype(bf16)
    score_out[...] = jnp.broadcast_to(score, (8, 128))


def pull_only_kernel(images_ref, lift_ref, kernel_ref, head_ref, copies_ref, score_ref, patch_ref):
    lift_half = lift_ref[...].astype(bf16)
    kernel_of = lambda t: kernel_ref[:, CH * t : CH * (t + 1)]
    slope, z_grad, _, score = critic_forward(images_ref[...], lift_half, kernel_of, head_ref[...], patch_ref)
    parts = row_parts(z_grad)
    pre_grad = lift_pullback(slope, parts, kernel_of)
    pull = (-8.0 * dot(lift_half, pre_grad, NT)[:, :FAKE]).astype(bf16)
    for j in range(8):
        copies_ref[j] = pull
    high = score.astype(bf16)
    middle = (score - high.astype(f32)).astype(bf16)
    low = (score - high.astype(f32) - middle.astype(f32)).astype(bf16)
    lane = lax.broadcasted_iota(jnp.int32, (C, 128), 1)
    three = jnp.where(lane == 0, high.astype(f32), jnp.where(lane == 1, middle.astype(f32), jnp.where(lane == 2, low.astype(f32), 0.0)))
    score_ref[...] = three.astype(bf16)


def moved_first_kernel(part_a, part_b, lift_out, kernel_out, head_out, patch_ref, half_ref):
    for t in range(TAPS):
        cols = slice(CH * t, CH * (t + 1))
        half_ref[t, :PART_A] = part_a[:, cols]
        half_ref[t, PART_A:] = part_b[:, cols]
    images = moved_images(part_b, 0)
    lift_half = part_b[2 * C :, KW + 128 : KW + 384]
    lane = part_b[2 * C :, KW + 384 :].astype(f32)
    head = jnp.concatenate([lane[:1], lane[16:17]], axis=1)
    kernel_of = lambda t: half_ref[t]
    slope, z_grad, head_grad, _ = critic_forward(images, lift_half, kernel_of, head, patch_ref)
    parts = row_parts(z_grad)
    pre_grad = lift_pullback(slope, parts, kernel_of)
    lift_out[...] = lift_half.astype(f32) - critic_rate * dot(images[:, :ROWS], pre_grad)
    head_out[...] = head - critic_rate * head_grad
    z_turned = turned(parts)
    for t in range(TAPS):
        kernel_out[:, CH * t : CH * (t + 1)] = kernel_of(t).astype(f32) - critic_rate * dot(z_turned[t // 3], patch_ref[t % 3])


def moved_second_kernel(part_b, lift_ref, kernel_ref, head_ref, lift_out, kernel_out, head_out, patch_ref, half_ref, new_ref, sems):
    for t in range(TAPS):
        half_ref[t] = kernel_ref[:, CH * t : CH * (t + 1)].astype(bf16)
    lift = lift_ref[...]
    head = head_ref[...]
    images = moved_images(part_b, 1)
    kernel_of = lambda t: half_ref[t]
    slope, z_grad, head_grad, _ = critic_forward(images, lift.astype(bf16), kernel_of, head, patch_ref)
    parts = row_parts(z_grad)
    pre_grad = lift_pullback(slope, parts, kernel_of)
    lift_out[...] = lift - critic_rate * dot(images[:, :ROWS], pre_grad)
    head_out[...] = head - critic_rate * head_grad
    z_turned = turned(parts)
    copies = []
    for t in range(TAPS):
        cols = slice(CH * t, CH * (t + 1))
        new_ref[t] = kernel_ref[:, cols] - critic_rate * dot(z_turned[t // 3], patch_ref[t % 3])
        copies.append(pltpu.make_async_copy(new_ref.at[t], kernel_out.at[:, cols], sems.at[t]))
        copies[t].start()
    for copy in copies:
        copy.wait()


def generator_step(total, latents, first, second):
    inner = exact_dot(latents, first, NT)
    gate = sigmoid(inner)
    second_grad = exact_dot(total, inner * gate)
    inner_grad = exact_dot(jnp.transpose(total), second) * (gate * (1.0 + inner * (1.0 - gate)))
    first_grad = exact_dot(jnp.transpose(inner_grad), latents)
    return first - generator_rate * first_grad, second - generator_rate * second_grad


def middle_kernel(pick_ref, own_ref, other_ref, noise_ref, first_ref, second_ref, pool_ref, images_ref, first_out, second_out):
    first, second = generator_step(own_ref[...].astype(f32) + other_ref[...].astype(f32), latents_of(noise_ref, 0), first_ref[...], second_ref[...])
    first_out[...] = first
    second_out[...] = second
    inner = exact_dot(latents_of(noise_ref, 1), first, NT)
    fakes = exact_dot(second, inner * sigmoid(inner), NT)
    put_images(images_ref, fakes, real_image(pool_ref, pick_ref, 1))


def last_kernel(place_ref, own_ref, other_ref, noise_ref, first_ref, second_ref, score_ref, first_out, second_out, own_out, scores_out):
    total = own_ref[:, :FAKE].astype(f32) + other_ref[:, :FAKE].astype(f32)
    first, second = generator_step(total, latents_of(noise_ref, 1), first_ref[...], second_ref[...])
    first_out[...] = first
    second_out[...] = second
    own = jnp.zeros((C, C), f32)
    for j in range(N_GRP):
        own = own + jnp.where(place_ref[0] == j, total[:, C * j : C * (j + 1)], 0.0)
    own_out[...] = own
    scores_out[0, 0] = jnp.max(score_ref[...])
    scores_out[0, 1] = jnp.sum(own_ref[:, FAKE:].astype(f32)[:1])


def vmem(*_):
    return pl.BlockSpec(memory_space=pltpu.VMEM)


def smem():
    return pl.BlockSpec(memory_space=pltpu.SMEM)


def call(kernel, name, outs, ins, scratch=(), scalars=0, work=0):
    return pl.pallas_call(
        kernel,
        name=name,
        out_shape=[jax.ShapeDtypeStruct(s, d) for s, d in outs],
        in_specs=[smem()] * scalars + [vmem()] * (len(ins) - scalars),
        out_specs=[vmem()] * len(outs),
        scratch_shapes=list(scratch),
        cost_estimate=pl.CostEstimate(flops=work, bytes_accessed=0, transcendentals=0) if work else None,
        compiler_params=pltpu.CompilerParams(vmem_limit_bytes=24 * 1024 * 1024),
    )(*ins)


def shifted(value, steps):
    count = lax.axis_size("loop")
    return lax.ppermute(value, "loop", [(s, (s + steps) % count) for s in range(count)])


def across(value):
    return lax.ppermute(value, "grp", [(m, m ^ 8) for m in range(N_GRP)])


def swap(copies):
    count = lax.axis_size("loop")
    groups = [[8 * i + j for j in range(8)] for i in range(2 * count)]
    return lax.all_to_all(copies, ("loop", "grp"), 0, 0, axis_index_groups=groups)


def together(*values):
    return lax.optimization_barrier(values)


PATCHES = pltpu.VMEM((3, ROWS, CH), bf16)
HALVES = pltpu.VMEM((TAPS, CH, CH), bf16)


def per_device(real_pool, real_pick, noise_latents, generator_in, generator_out, critic_lift, critic_kernel, critic_head):
    pool = real_pool[0, 0]
    pick = real_pick[0, 0, :, 0]
    first, second = generator_in[0], generator_out[0]
    lift = jnp.swapaxes(critic_lift[0, 0], 0, 1)
    kernel = critic_kernel[0, 0]
    head = critic_head[0, 0][None]

    place = lax.axis_index("grp").astype(jnp.int32)[None]
    own_noise = jnp.swapaxes(noise_latents[0], 1, 2).reshape(ROUNDS * C, 128)
    other_noise = across(own_noise)
    small = (first, second, pool, lift, head, own_noise)
    part_a, first, second, pool, lift, head, own_noise = pl.pallas_call(
        stage_kernel,
        name="stage",
        out_shape=[jax.ShapeDtypeStruct((PART_A, KW), bf16)] + [jax.ShapeDtypeStruct(x.shape, x.dtype) for x in small],
        in_specs=[pl.BlockSpec(memory_space=pltpu.HBM)] * 7,
        out_specs=[vmem()] * 7,
        scratch_shapes=[pltpu.VMEM((PART_A, KW), f32), pltpu.SemaphoreType.DMA((7,))],
        compiler_params=pltpu.CompilerParams(vmem_limit_bytes=56 * 1024 * 1024),
    )(kernel, *small)
    (copies,) = call(
        noise_copies_kernel, "noise_copies", [((8, 4 * C, 128), bf16)], (place, own_noise, other_noise), scalars=1, work=COPY_WORK
    )
    part_a, copies = together(part_a, copies)
    moved_a = shifted(part_a, 2)
    noise = swap(copies)
    (images,) = call(
        generate_kernel, "make_fakes", [((C, WIDE), bf16)], (pick, noise, first, second, pool), scalars=1
    )
    copies, lift_1, kernel_1, head_1, score_0, part_b = call(
        first_step_kernel,
        "first_step",
        [((8, C, FAKE), bf16), ((C, CH), f32), ((CH, KW), bf16), ((1, CH), f32), ((8, 128), f32), ((PART_B, KW + EXTRA), bf16)],
        (images, lift, kernel, head),
        (PATCHES, HALVES),
        work=FIRST_WORK,
    )
    (partial,) = call(sum_kernel, "sum_first", [((C, FAKE), bf16)], (swap(copies),))
    other = across(partial)
    own_images, first_1, second_1 = call(
        middle_kernel,
        "generator_step",
        [((C, WIDE), bf16), ((CH, 128), f32), ((C, CH), f32)],
        (pick, partial, other, noise, first, second, pool),
        scalars=1,
    )
    ahead_images = shifted(own_images, -1)
    (part_b,) = call(
        add_images_kernel, "add_images", [((PART_B, KW + EXTRA), bf16)], (ahead_images, part_b)
    )
    part_b, ahead_images, moved_a = together(part_b, ahead_images, moved_a)
    moved_b = shifted(part_b, 2)
    copies, score_1 = call(
        pull_only_kernel,
        "second_pull",
        [((8, C, FAKE), bf16), ((C, 128), bf16)],
        (ahead_images, lift_1, kernel_1, head_1),
        (PATCHES,),
    )
    (partial,) = call(scored_sum_kernel, "sum_second", [((C, WIDE), bf16)], (swap(copies), score_1))
    same = shifted(partial, 1)

    moved_lift, moved_kernel, moved_head = call(
        moved_first_kernel,
        "moved_first",
        [((C, CH), f32), ((CH, KW), f32), ((1, CH), f32)],
        (moved_a, moved_b),
        (PATCHES, HALVES),
    )
    moved_lift, same = together(moved_lift, same)
    cross = across(same)
    lift_2, kernel_2, head_2 = pl.pallas_call(
        moved_second_kernel,
        name="moved_second",
        out_shape=[jax.ShapeDtypeStruct(x, f32) for x in ((C, CH), (CH, KW), (1, CH))],
        in_specs=[vmem()] * 4,
        out_specs=[vmem(), pl.BlockSpec(memory_space=pltpu.HBM), vmem()],
        scratch_shapes=[PATCHES, HALVES, pltpu.VMEM((TAPS, CH, CH), f32), pltpu.SemaphoreType.DMA((TAPS,))],
        compiler_params=pltpu.CompilerParams(vmem_limit_bytes=24 * 1024 * 1024),
    )(moved_b, moved_lift, moved_kernel, moved_head)
    first_2, second_2, own_grad, scores = pl.pallas_call(
        last_kernel,
        name="generator_last",
        out_shape=[
            jax.ShapeDtypeStruct((CH, 128), f32),
            jax.ShapeDtypeStruct((C, CH), f32),
            jax.ShapeDtypeStruct((C, C), f32),
            jax.ShapeDtypeStruct((1, ROUNDS), f32),
        ],
        in_specs=[smem()] + [vmem()] * 6,
        out_specs=[vmem()] * 3 + [smem()],
        compiler_params=pltpu.CompilerParams(vmem_limit_bytes=24 * 1024 * 1024),
    )(place, same, cross, noise, first_1, second_1, score_0)
    return (
        jnp.swapaxes(lift_2, 0, 1)[None, None],
        kernel_2[None, None],
        head_2.reshape(1, 1, CH),
        first_2[None],
        second_2[None],
        own_grad[None],
        scores.reshape(1, 1, ROUNDS, 1),
    )


def solution(mesh):
    return jax.shard_map(
        per_device,
        mesh=mesh,
        in_specs=(
            P("loop", "grp", None, None, None),
            P("loop", "grp", None, None),
            P("loop", None, None, "grp"),
            P("loop", None, None),
            P("loop", None, None),
            P("loop", "grp", None, None),
            P("loop", "grp", None, None),
            P("loop", "grp", None),
        ),
        out_specs=(
            P("loop", "grp", None, None),
            P("loop", "grp", None, None),
            P("loop", "grp", None),
            P("loop", None, None),
            P("loop", None, None),
            P("loop", None, "grp"),
            P("loop", "grp", None, None),
        ),
        check_vma=False,
    )
```
